512 devices in a mesh: expert: 64 (over y, z), head: 8 (over x, core).
Axes of the slice: x: 4, y: 8, z: 8, core: 2. Of those that a mesh axis runs over, the one named last changes fastest.
Arguments:
- queries: bfloat16 [2, 2048, 2048], P(None, 'expert', 'head'), may hold values from -12 to 12
- cache_band: bfloat16 [2048, 128, 1024], P('expert', None, 'head'), may hold values from -12 to 12
- new_kv: bfloat16 [2, 2048, 1024], P(None, 'expert', 'head'), may hold values from -4 to 4
- cache_lengths: int32 [2048], P('expert'), may hold values from 1 to 8192
- sink_logits: float32 [32], P('head'), may hold values from -6 to 6
- o_weight: bfloat16 [2048, 2880], P('head'), may hold values from -0.75 to 0.75
- residual: bfloat16 [2, 2048, 2880], P(None, 'expert', 'head'), may hold values from -54 to 54
- norm_gain: float32 [2880], replicated, may hold values from 0.1 to 1.9
- route_logits: float32 [2, 2048, 4], P(None, 'expert'), may hold values from -8 to 400
- routes: int32 [2, 2048, 4], P(None, 'expert'), may hold values from 0 to 31, as said below
- old_experts: int32 [32], replicated, may hold values from 0 to 31, each once
- new_experts: int32 [32], replicated, may hold values from 0 to 31, each once
- train_gate_up: bfloat16 [32, 2880, 2, 2048], P(None, 'expert', None, 'head'), may hold values from -0.21875 to 0.21875
- train_down: bfloat16 [32, 2880, 2048], P(None, 'expert', 'head'), may hold values from -0.125 to 0.125
Outputs:
- layer_out: bfloat16 [2, 2048, 2880], P(None, 'expert', 'head')
- synced_down: bfloat16 [64, 2880, 1024], P('expert', None, 'head')
The draws below stay inside these ranges and needn't reach their ends.
Inputs may be any that keep to these rules, and one draw needn't show every extreme that they name: `old_experts`: a permutation. `new_experts`: a permutation. `routes`: each row names 4 different experts; in each step and each aligned block of 32 sequences (one device's rows) no expert is named by more than 8 rows, and in each step one expert is named by exactly 8 rows of every block.
All inputs are finite; a program needn't handle non-finite values.
Results may differ from the reference program's by a relative error of at most 0.028.
Values may be sent and summed in bfloat16 or wider, within the bound.
A program may use at most 128 MiB of HBM per device.

```python
import math
import jax
import jax.numpy as jnp
from jax import lax

D = 2880
FF = 2048
QH = 32
KVH = 8
HD = 64
WINDOW = 128
CACHE = 8192
TOP = 4
STEPS = 2
SEQ_DEV = 32
EXPERTS = 32
SEQS = 2048
CAP = 8
FFQ = 128
N_EXPERT = 64
N_HEAD = 8


def draw_queries(key, part):
    key = jax.random.fold_in(key, 1)
    block_shape = (STEPS, SEQS, KVH, QH // KVH, HD)
    base_values = jnp.clip(jax.random.normal(key, block_shape, jnp.float32), -4.0, 4.0)
    return base_values.reshape(STEPS, SEQS, QH * HD).astype(jnp.bfloat16)


def draw_cache_band(key, part):
    key = jax.random.fold_in(key, 2)
    block_shape = (SEQS, WINDOW, KVH, 2, HD)
    base_values = jnp.clip(jax.random.normal(key, block_shape, jnp.float32), -4.0, 4.0)
    return base_values.reshape(SEQS, WINDOW, KVH * 2 * HD).astype(jnp.bfloat16)


def draw_route_logits(key, part):
    key = jax.random.fold_in(key, 3)
    first_key = jax.random.fold_in(key, 0)
    base_values = jnp.clip(1.5 * jax.random.normal(first_key, (STEPS, SEQS, TOP), jnp.float32), -8.0, 8.0)
    return base_values


def draw_residual(key, part):
    key = jax.random.fold_in(key, 4)
    first_key, second_key, third_key = jax.random.split(key, 3)
    row_scale = jnp.exp(jax.random.uniform(second_key, (STEPS, SEQS, 1), jnp.float32, math.log(0.3), math.log(3.0)))
    col_scale = jnp.exp(jax.random.uniform(third_key, (D,), jnp.float32, math.log(0.3), math.log(3.0)))
    col_scale = col_scale * (0.5 + jnp.arange(D, dtype=jnp.float32) / D)
    base_values = jnp.clip(jax.random.normal(first_key, (STEPS, SEQS, D), jnp.float32), -4.0, 4.0)
    return (base_values * row_scale * col_scale).astype(jnp.bfloat16)


def draw_cache_lengths(key, part):
    key = jax.random.fold_in(key, 5)
    first_key, second_key, third_key, fourth_key = jax.random.split(key, 4)
    short_lengths = jax.random.randint(first_key, (SEQS,), 1, 2 * WINDOW)
    long_lengths = jax.random.randint(second_key, (SEQS,), 1, CACHE + 1)
    coin_flip = jax.random.randint(third_key, (SEQS,), 0, 2)
    lengths = jnp.where(coin_flip == 0, short_lengths, long_lengths)
    end_rows = jax.random.permutation(fourth_key, SEQS)
    lengths = lengths.at[end_rows[0]].set(CACHE).at[end_rows[1]].set(1)
    return lengths.astype(jnp.int32)


def draw_routes(key, part):
    key = jax.random.fold_in(key, 6)
    blocks = SEQS // SEQ_DEV
    others = EXPERTS - 1
    spacing = others // 4

    def one_step(step_key):
        relabel_key, block_key = jax.random.split(step_key)
        relabel = jax.random.permutation(relabel_key, EXPERTS).astype(jnp.int32)

        def one_block(each_key):
            first_key, second_key, third_key = jax.random.split(each_key, 3)
            row_order = jax.random.permutation(first_key, SEQ_DEV)
            hot_row = row_order < CAP
            shift_value = jax.random.randint(second_key, (), 0, others)
            spread = (jax.random.permutation(third_key, SEQ_DEV) + shift_value) % others
            cycle_slot = 1 + (spread[:, None] + jnp.arange(TOP)[None, :] * spacing) % others
            with_hot = jnp.concatenate([jnp.zeros((SEQ_DEV, 1), cycle_slot.dtype), cycle_slot[:, :TOP - 1]], axis=1)
            return relabel[jnp.where(hot_row[:, None], with_hot, cycle_slot)]
        return jax.vmap(one_block)(jax.random.split(block_key, blocks)).reshape(SEQS, TOP)
    return jax.vmap(one_step)(jax.random.split(key, STEPS)).astype(jnp.int32)


def block_scale(rng, extent, cuts, low, largest):
    level, own = 1.0, jax.random.fold_in(rng, 6)
    for dim, parts in cuts:
        draws = jnp.exp(jax.random.uniform(jax.random.fold_in(own, dim), (parts,), jnp.float32, low / len(cuts), largest / len(cuts)))
        level = level * jnp.repeat(draws, extent[dim] // parts).reshape([-1 if axis == dim else 1 for axis in range(len(extent))])
    return level


def noise(own_key, shape, scale, bound, cuts=(), kind=jnp.bfloat16):
    drawn = scale * jax.random.normal(own_key, shape, jnp.float32)
    if cuts:
        drawn = drawn * block_scale(own_key, shape, cuts, -0.22, 0.18)
    return jnp.clip(drawn, -bound, bound).astype(kind)


def setup_inputs(seed: int = 0) -> dict:
    seeds = jax.random.split(jax.random.key(seed), 15)
    queries = draw_queries(jax.random.fold_in(seeds[14], 71), 0)
    cache_band = draw_cache_band(jax.random.fold_in(seeds[14], 71), 0)
    new_kv = noise(seeds[2], (STEPS, SEQS, 2 * KVH * HD), 1.0, 4.0, ((1, 64), (2, 8)))
    cache_lengths = draw_cache_lengths(jax.random.fold_in(seeds[14], 71), 0)
    sink_logits = noise(seeds[4], (QH,), 1.5, 6.0, ((0, 8),), jnp.float32)
    o_weight = noise(seeds[5], (QH * HD, D), HD ** -0.5, 0.75, ((0, 8),))
    residual = draw_residual(jax.random.fold_in(seeds[14], 71), 0)
    norm_gain = jnp.clip(1.0 + 0.18 * jax.random.normal(seeds[7], (D,), jnp.float32), 0.1, 1.9)
    route_logits = draw_route_logits(jax.random.fold_in(seeds[14], 71), 0)
    routes = draw_routes(jax.random.fold_in(seeds[14], 71), 0)
    old_experts = jax.random.permutation(seeds[10], EXPERTS).astype(jnp.int32)
    new_experts = jax.random.permutation(seeds[11], EXPERTS).astype(jnp.int32)
    train_gate_up = noise(seeds[12], (EXPERTS, D, 2, FF), (D // 4) ** -0.5, 0.21875, ((1, 64), (3, 8)))
    train_down = noise(seeds[13], (EXPERTS, D, FF), FF ** -0.5, 0.125, ((1, 64), (2, 8)))
    return {"queries": queries, "cache_band": cache_band, "new_kv": new_kv, "cache_lengths": cache_lengths, "sink_logits": sink_logits, "o_weight": o_weight, "residual": residual, "norm_gain": norm_gain, "route_logits": route_logits, "routes": routes, "old_experts": old_experts, "new_experts": new_experts, "train_gate_up": train_gate_up, "train_down": train_down}


EPSILON = 1e-05

def attention_step(step_index, queries, extended, cache_lengths, sink_logits):
    group_size = QH // KVH
    query_rows = queries[step_index].astype(jnp.float32).reshape(SEQS, KVH, group_size, HD)
    visible_slots = extended[:, step_index + 1:step_index + 1 + WINDOW].astype(jnp.float32)
    visible_slots = visible_slots.reshape(SEQS, WINDOW, KVH, 2, HD)
    key_rows = visible_slots[:, :, :, 0, :]
    value_rows = visible_slots[:, :, :, 1, :]
    scores = jnp.einsum('svgd,swvd->svgw', query_rows, key_rows) * HD ** (-0.5)
    slot_index = step_index + 1 + jnp.arange(WINDOW, dtype=jnp.int32)
    visible = slot_index[None, :] >= (WINDOW - cache_lengths)[:, None]
    scores = jnp.where(visible[:, None, None, :], scores, -1e+30)
    sink_part = sink_logits.astype(jnp.float32).reshape(KVH, group_size)[None, :, :, None]
    row_top = jnp.maximum(lax.optimization_barrier(jnp.max(scores, axis=-1, keepdims=True)), sink_part)
    raised = jnp.exp(scores - row_top)
    sum_raised = lax.optimization_barrier(jnp.sum(raised, axis=-1, keepdims=True)) + jnp.exp(sink_part - row_top)
    probabilities = (raised / sum_raised).astype(jnp.bfloat16)
    mixed_values = jnp.einsum('svgw,swvd->svgd', probabilities.astype(jnp.float32), value_rows)
    return mixed_values.astype(jnp.bfloat16).reshape(SEQS, QH * HD)

def position_table(old_experts):
    counter = jnp.arange(EXPERTS, dtype=jnp.int32)
    return lax.optimization_barrier(jnp.sum(jnp.where(old_experts[None, :] == counter[:, None], counter[None, :], 0), axis=1)).astype(jnp.int32)

def expert_outputs(normed, route_step, old_experts, train_gate_up, train_down):
    capacity = N_EXPERT * CAP
    flat_routes = route_step.reshape(-1)
    onehot = (flat_routes[:, None] == jnp.arange(EXPERTS, dtype=jnp.int32)[None, :]).astype(jnp.int32)
    route_rank = lax.optimization_barrier(jnp.sum((jnp.cumsum(onehot, axis=0) - onehot) * onehot, axis=1)).astype(jnp.int32)
    token_index = jnp.arange(SEQS * TOP, dtype=jnp.int32) // TOP
    slot_table = jnp.full((EXPERTS, capacity), SEQS, dtype=jnp.int32).at[flat_routes, route_rank].set(token_index)
    padded = jnp.concatenate([normed, jnp.zeros((1, D), normed.dtype)], axis=0)
    slices = FF // N_HEAD

    def run_expert(position):
        token_rows = padded[slot_table[old_experts[position]]].astype(jnp.float32)
        weights_in = train_gate_up[position].astype(jnp.float32)
        gate_value = jnp.dot(token_rows, weights_in[:, 0, :], precision=lax.Precision.HIGHEST)
        up_value = jnp.dot(token_rows, weights_in[:, 1, :], precision=lax.Precision.HIGHEST)
        gate_value = jnp.minimum(gate_value, 7.0)
        up_value = jnp.clip(up_value, -7.0, 7.0)
        active = ((up_value + 1.0) * gate_value * jax.nn.sigmoid(1.702 * gate_value)).astype(jnp.bfloat16)
        pieces = jnp.einsum('rhf,dhf->rhd', active.astype(jnp.float32).reshape(capacity, N_HEAD, slices), train_down[position].astype(jnp.float32).reshape(D, N_HEAD, slices), precision=lax.Precision.HIGHEST)
        rounded = lax.optimization_barrier(pieces.astype(jnp.bfloat16))
        return lax.optimization_barrier(jnp.sum(rounded.astype(jnp.float32), axis=1))
    results = lax.map(run_expert, jnp.arange(EXPERTS, dtype=jnp.int32))
    picked = results[position_table(old_experts)[flat_routes], route_rank]
    return picked.reshape(SEQS, TOP, D)

def reference(queries, cache_band, new_kv, cache_lengths, sink_logits, o_weight, residual, norm_gain, route_logits, routes, old_experts, new_experts, train_gate_up, train_down):
    extended = jnp.concatenate([cache_band, jnp.swapaxes(new_kv, 0, 1)], axis=1)
    outputs = []
    for step_index in range(STEPS):
        attended = attention_step(step_index, queries, extended, cache_lengths, sink_logits)
        hidden = residual[step_index].astype(jnp.float32) + jnp.dot(attended, o_weight, preferred_element_type=jnp.float32)
        mean_square = lax.optimization_barrier(jnp.mean(hidden * hidden, axis=1, keepdims=True))
        normed = (hidden * lax.rsqrt(mean_square + EPSILON) * norm_gain).astype(jnp.bfloat16)
        route_weight = jax.nn.softmax(route_logits[step_index].astype(jnp.float32), axis=-1)
        expert_out = expert_outputs(normed, routes[step_index], old_experts, train_gate_up, train_down)
        combined = hidden + lax.optimization_barrier(jnp.sum(route_weight[:, :, None] * expert_out, axis=1))
        outputs.append(combined.astype(jnp.bfloat16))
    layer_out = jnp.stack(outputs)
    serving_pos = position_table(old_experts)[new_experts]
    moved_weights = train_down[serving_pos].reshape(EXPERTS, D, N_HEAD, 2, FFQ)
    synced_down = jnp.transpose(moved_weights, (0, 3, 1, 2, 4)).reshape(2 * EXPERTS, D, N_HEAD * FFQ)
    return (layer_out, synced_down)
```

```python
import functools
import jax
import jax.numpy as jnp
from jax import lax
from jax.experimental import pallas as pl
from jax.experimental.pallas import tpu as pltpu
from jax.sharding import PartitionSpec as P

HD = 64
TOP = 4
STEPS = 2
GROUP = 4
CAP = 8
ROWS = STEPS * CAP
EPSILON = 1e-05
CHUNKS = 4
MESH = pl.DeviceIdType.MESH
BF = jnp.bfloat16
F32 = jnp.float32
EXACT = lax.Precision.HIGHEST


def iota(shape, dim):
    return lax.broadcasted_iota(jnp.int32, shape, dim)


def dot(a, b, dims=((1,), (0,)), precision=None):
    return lax.dot_general(a, b, (dims, ((), ())), preferred_element_type=F32, precision=precision)


def column(row, size):
    eye = iota((size, size), 0) == iota((size, size), 1)
    return jnp.sum(jnp.where(eye, row, 0.0), axis=1, keepdims=True)


def log2(n):
    assert n & (n - 1) == 0
    return n.bit_length() - 1


def kernel(
    n_expert,
    n_head,
    pos_ref,
    new_ref,
    len_ref,
    sink_ref,
    logit_ref,
    route_ref,
    gain_ref,
    query_ref,
    band_ref,
    new_kv_ref,
    o_ref,
    residual_ref,
    gate_up_ref,
    down_ref,
    out_ref,
    sync_ref,
    down_f,
    gu_out,
    dn_out,
    gu_in,
    dn_in,
    part_out,
    part_in,
    tok_out,
    tok_all,
    y_out,
    y_in,
    z_out,
    z_in,
    ret_out,
    ret_in,
    sync_f,
    sem,
    ag_sem,
    rs_sem,
):
    experts = n_expert // 2
    n_chip = n_head // 2
    seqs = query_ref.shape[1]
    cols = STEPS * seqs
    block = gate_up_ref.shape[1]
    padded = gu_in.shape[1]
    share = residual_ref.shape[2]
    per_head = n_expert // n_head
    wide = per_head * padded
    width = n_head * share
    half = gate_up_ref.shape[3] // 2
    seq_bits = log2(seqs)

    me = lax.axis_index("expert")
    head = lax.axis_index("head")
    core = lax.rem(head, 2)
    chip = head // 2
    mate = head + 1 - 2 * core
    my_slot = me // 2
    partner = me + 1 - 2 * lax.rem(me, 2)
    my_half = lax.rem(me, 2)

    barrier = pltpu.get_barrier_semaphore()

    def greet_expert(i, carry):
        pl.semaphore_signal(
            barrier, inc=1, device_id=(lax.rem(me + i, n_expert), head), device_id_type=MESH
        )
        return carry

    def greet_head(i, carry):
        pl.semaphore_signal(
            barrier, inc=1, device_id=(me, lax.rem(head + i, n_head)), device_id_type=MESH
        )
        return carry

    lax.fori_loop(1, n_expert, greet_expert, 0)
    lax.fori_loop(1, n_head, greet_head, 0)

    for p in range(2):
        down_f[p] = (
            down_ref[:, :, p * half : (p + 1) * half].astype(F32).reshape(block * experts, half)
        )
    pad = padded - block
    tail = padded - 16 if padded >= 16 else 0
    gu_out[:, :, tail:, :] = jnp.zeros((experts, 2, padded - tail, 2 * half), BF)
    dn_out[:, :, tail:, :] = jnp.zeros((experts, 2, padded - tail, half), BF)

    pl.semaphore_wait(barrier, n_expert + n_head - 2)

    GU_S, GU_R, DN_S, DN_R, PART_S, PART_R, TOK_S, TOK_R, RET_S, RET_R, AG_S, Y_S, Z_S = range(13)

    def send(src, dst, e, h, s, r):
        pltpu.make_async_remote_copy(
            src_ref=src,
            dst_ref=dst,
            send_sem=s,
            recv_sem=r,
            device_id=(e, h),
            device_id_type=MESH,
        ).start()

    def drain(ref, s):
        pltpu.make_async_copy(ref, ref, s).wait()

    def prepare_gate_up(slot):
        index = pos_ref[slot]
        for p in range(2):
            for c in range(2):
                gu_out[slot, p, :block, c * half : (c + 1) * half] = gate_up_ref[
                    index, :, c, p * half : (p + 1) * half
                ]

    def prepare_down(slot):
        index = pos_ref[slot]
        for p in range(2):
            dn_out[slot, p, :block, :] = down_f[
                p, pl.ds(index, block, stride=experts), :
            ].astype(BF)

    def send_gate_up(i, carry):
        slot = lax.rem(my_slot + i, experts)
        prepare_gate_up(slot)
        for p in range(2):
            send(gu_out.at[slot, p], gu_in.at[me], 2 * slot + p, head, sem.at[GU_S], sem.at[GU_R])
        return carry

    def send_down(i, carry):
        slot = lax.rem(my_slot + i, experts)
        prepare_down(slot)
        for p in range(2):
            send(dn_out.at[slot, p], dn_in.at[me], 2 * slot + p, head, sem.at[DN_S], sem.at[DN_R])
        return carry

    prepare_gate_up(my_slot)
    prepare_down(my_slot)
    send(gu_out.at[my_slot, 1 - my_half], gu_in.at[me], partner, head, sem.at[GU_S], sem.at[GU_R])
    send(dn_out.at[my_slot, 1 - my_half], dn_in.at[me], partner, head, sem.at[DN_S], sem.at[DN_R])
    gu_in[me] = gu_out[my_slot, my_half]
    dn_in[me] = dn_out[my_slot, my_half]
    first_batch = experts // 2
    lax.fori_loop(1, first_batch, send_gate_up, 0)

    lanes = 2 * HD
    rows = STEPS * GROUP * seqs
    r_id = iota((rows, cols), 0)
    c_id = iota((rows, cols), 1)
    same = ((r_id >> 3) == (c_id & (seqs - 1))) & (((r_id >> 2) & 1) == (c_id >> seq_bits))
    rt_id = iota((cols, rows), 1)
    ct_id = iota((cols, rows), 0)
    same_t = ((rt_id >> 3) == (ct_id & (seqs - 1))) & (((rt_id >> 2) & 1) == (ct_id >> seq_bits))
    flat_q = query_ref[...].reshape(cols, GROUP * HD)
    spread_q = jnp.zeros((rows, lanes), F32)
    for g in range(GROUP):
        k_id = iota((GROUP * HD, lanes), 0)
        l_id = iota((GROUP * HD, lanes), 1)
        pick = ((k_id == g * HD + l_id) & (l_id < HD)).astype(BF)
        part = dot(flat_q, pick).astype(BF)
        spread_q += dot((same & ((r_id & 3) == g)).astype(BF), part)
    repeat = ((iota((rows, seqs), 0) >> 3) == iota((rows, seqs), 1)).astype(BF)
    fresh = [dot(repeat, new_kv_ref[s]) for s in range(STEPS)]
    row_s = (iota((rows, 1), 0) >> 2) & 1
    row_g = iota((rows, 1), 0) & 3
    lengths = jnp.sum(
        jnp.where(
            (iota((rows, seqs), 0) >> 3) == iota((rows, seqs), 1), len_ref[...].astype(F32), 0.0
        ),
        axis=1,
        keepdims=True,
    )
    sink = jnp.sum(
        jnp.where(row_g == iota((rows, GROUP), 1), sink_ref[...], 0.0), axis=1, keepdims=True
    )
    scale = HD**-0.5
    batched = (((2,), (2,)), ((0,), (0,)))
    scores = (
        lax.dot_general(
            spread_q.reshape(seqs, STEPS * GROUP, lanes).astype(BF),
            band_ref[...],
            batched,
            preferred_element_type=F32,
        ).reshape(rows, -1)
        * scale
    )
    window = band_ref.shape[1]
    w_id = iota((rows, window), 1)
    kept = (w_id >= row_s + 1) & (w_id.astype(F32) >= window - lengths)
    scores = jnp.where(kept, scores, -1e30)
    new_scores = [
        jnp.sum(spread_q * fresh[s], axis=1, keepdims=True) * scale for s in range(STEPS)
    ]
    new_scores[1] = jnp.where(row_s == 1, new_scores[1], -1e30)
    top = jnp.maximum(jnp.max(scores, axis=1, keepdims=True), sink)
    top = jnp.maximum(jnp.maximum(top, new_scores[0]), new_scores[1])
    raised = jnp.exp(scores - top)
    new_raised = [jnp.exp(n - top) for n in new_scores]
    total = jnp.sum(raised, axis=1, keepdims=True) + jnp.exp(sink - top)
    total = total + new_raised[0] + new_raised[1]
    probs = (raised / total).reshape(seqs, STEPS * GROUP, window).astype(BF)
    mixed = lax.dot_general(
        probs, band_ref[...], (((2,), (1,)), ((0,), (0,))), preferred_element_type=F32
    ).reshape(rows, lanes)
    for s in range(STEPS):
        mixed += (new_raised[s] / total).astype(BF).astype(F32) * fresh[s]
    mixed = mixed.astype(BF)
    attended = jnp.zeros((cols, GROUP * HD), F32)
    for g in range(GROUP):
        l_id = iota((lanes, GROUP * HD), 0)
        k_id = iota((lanes, GROUP * HD), 1)
        pick = ((k_id - g * HD == l_id - HD) & (l_id >= HD)).astype(BF)
        part = dot(mixed, pick).astype(BF)
        attended += dot((same_t & ((rt_id & 3) == g)).astype(BF), part)
    attended = attended.astype(BF)

    for j in range(n_head):
        part_out[j] = dot(attended, o_ref[j * share : (j + 1) * share, :], ((1,), (1,))).astype(BF)

    def send_part(i, carry):
        to = lax.rem(head + i, n_head)
        send(part_out.at[to], part_in.at[head], me, to, sem.at[PART_S], sem.at[PART_R])
        return carry

    lax.fori_loop(1, n_head, send_part, 0)
    part_in[head] = part_out[head]

    new_col = column(new_ref[...].astype(F32), experts)
    logits = [logit_ref[j : j + 1, :] for j in range(TOP)]
    highest = functools.reduce(jnp.maximum, logits)
    powers = [jnp.exp(l - highest) for l in logits]
    power_sum = functools.reduce(jnp.add, powers)
    member = jnp.zeros((experts, cols), F32)
    weight = jnp.zeros((experts, cols), F32)
    for j in range(TOP):
        hit = (route_ref[j : j + 1, :].astype(F32) == new_col).astype(F32)
        member += hit
        weight += hit * (powers[j] / power_sum)
    u0 = iota((cols, cols), 0)
    u1 = iota((cols, cols), 1)
    before = ((u0 < u1) & ((u0 >> seq_bits) == (u1 >> seq_bits))).astype(BF)
    rank = dot(member.astype(BF), before)
    slots = experts * ROWS
    of_slot = ((iota((slots, experts), 0) >> 4) == iota((slots, experts), 1)).astype(BF)
    member_rows = dot(of_slot, member.astype(BF))
    rank_rows = dot(of_slot, rank.astype(BF))
    i_id = iota((slots, cols), 0)
    place = (
        member_rows
        * (rank_rows == (i_id & 7).astype(F32)).astype(F32)
        * (((i_id >> 3) & 1) == (iota((slots, cols), 1) >> seq_bits)).astype(F32)
    )
    combine = dot(of_slot.astype(F32), weight, precision=EXACT) * place

    drain(part_in.at[pl.ds(0, n_head - 1)], sem.at[PART_R])
    hidden = residual_ref[...].reshape(cols, share).astype(F32)
    for j in range(n_head):
        hidden += part_in[j].astype(F32)
    squares = jnp.sum(hidden * hidden, axis=1, keepdims=True)
    lane = iota((share, wide), 1)
    stretch = jnp.zeros((share, wide), F32)
    gap = jnp.zeros((share, wide), jnp.int32)
    for b in range(1, per_head):
        gap += pad * (iota((share, wide), 0) >= b * block).astype(jnp.int32)
    stretch = (iota((share, wide), 0) + gap == lane).astype(BF)
    gained = (hidden * gain_ref[pl.ds(head, 1), :]).astype(BF)
    token = dot(gained, stretch)
    high = squares.astype(BF).astype(F32)
    low = (squares - high).astype(BF).astype(F32)
    lane = iota((cols, wide), 1)
    token = jnp.where(lane == block, high, jnp.where(lane == block + 1, low, token)).astype(BF)
    tok_out[...] = dot(place.astype(BF), token).astype(BF).reshape(experts, ROWS, wide)

    def send_token(i, carry):
        slot = lax.rem(my_slot + i, experts)
        for p in range(2):
            send(
                tok_out.at[slot],
                tok_all.at[head, me],
                2 * slot + p,
                head,
                sem.at[TOK_S],
                sem.at[TOK_R],
            )
        return carry

    send(tok_out.at[my_slot], tok_all.at[head, me], partner, head, sem.at[TOK_S], sem.at[TOK_R])
    tok_all[head, me] = tok_out[my_slot]
    lax.fori_loop(1, experts, send_token, 0)

    lax.fori_loop(first_batch, experts, send_gate_up, 0)
    lax.fori_loop(1, experts, send_down, 0)

    drain(tok_all.at[head, pl.ds(0, n_expert - 1)], sem.at[TOK_R])
    per = n_expert // CHUNKS

    def chunk(k):
        return pl.ds(k * per, per)

    for k in range(CHUNKS):
        for d in range(1, n_chip):
            to = 2 * lax.rem(chip + d, n_chip) + core
            view = tok_all.at[head, chunk(k)]
            send(view, view, me, to, sem.at[AG_S], ag_sem.at[k, head])
        view = tok_all.at[head, chunk(k)]
        send(view, view, me, mate, sem.at[AG_S], ag_sem.at[k, head])
    for k in range(CHUNKS):
        for d in range(1, n_chip):
            source = 2 * lax.rem(chip + n_chip - d, n_chip) + core
            view = tok_all.at[source, chunk(k)]
            drain(view, ag_sem.at[k, source])
            send(view, view, me, mate, sem.at[AG_S], ag_sem.at[k, source])

    drain(gu_in.at[pl.ds(0, n_expert - 1)], sem.at[GU_R])
    drain(dn_in.at[pl.ds(0, n_expert - 1)], sem.at[DN_R])

    size = per * ROWS
    q_id = iota((wide, half), 0)
    pick = ((q_id == block) | (q_id == block + 1)).astype(BF)

    def run(k):
        for x in range(n_chip):
            source = 2 * x + 1 - core
            drain(tok_all.at[source, chunk(k)], ag_sem.at[k, source])
        acc = jnp.zeros((size, 2 * half), F32)
        norm = jnp.zeros((size, half), F32)
        for j in range(0, n_head, 2):
            pair = [tok_all[j + i, chunk(k)].reshape(size, wide) for i in range(2)]
            weights = gu_in[per_head * j : per_head * (j + 2)].reshape(2 * wide, 2 * half)
            acc += dot(jnp.concatenate(pair, axis=1), weights)
            for one in pair:
                norm += dot(one[:, : min(wide, 128)], pick[: min(wide, 128)])
        norm = lax.rsqrt(norm * (1.0 / width) + EPSILON)
        gate = jnp.minimum(acc[:, :half] * norm, 7.0)
        up = jnp.clip(acc[:, half:] * norm, -7.0, 7.0)
        active = ((up + 1.0) * gate * jax.nn.sigmoid(1.702 * gate)).astype(BF)
        for j in range(n_head):
            weights = dn_in[per_head * j : per_head * (j + 1)].reshape(wide, half)
            y = dot(active, weights, ((1,), (1,))).astype(BF)
            y_out[j // 2, j % 2, chunk(k)] = y.reshape(per, ROWS, wide)
        send(
            y_out.at[:, 1 - core, chunk(k)],
            y_in.at[:, chunk(k)],
            me,
            mate,
            sem.at[Y_S],
            rs_sem.at[k, 0],
        )

    def add_cores(k):
        drain(y_in.at[:, chunk(k)], rs_sem.at[k, 0])
        for d in range(n_chip):
            to = lax.rem(chip + d, n_chip)
            z = y_out[to, core, chunk(k)].astype(F32) + y_in[to, chunk(k)].astype(F32)
            z_out[to, chunk(k)] = z.astype(BF)
            if d > 0:
                send(
                    z_out.at[to, chunk(k)],
                    z_in.at[d - 1, chunk(k)],
                    me,
                    2 * to + core,
                    sem.at[Z_S],
                    rs_sem.at[k, d],
                )

    def add_chips(k):
        total = z_out[chip, chunk(k)].astype(F32)
        for d in range(1, n_chip):
            drain(z_in.at[d - 1, chunk(k)], rs_sem.at[k, d])
            total += z_in[d - 1, chunk(k)].astype(F32)
        ret_out[chunk(k)] = total.astype(BF)

        def give_back(i, carry):
            to = k * per + lax.rem(me + i, per)

            @pl.when(to != me)
            def _():
                send(ret_out.at[to], ret_in.at[me], to, head, sem.at[RET_S], sem.at[RET_R])

            @pl.when(to == me)
            def _():
                ret_in[me] = ret_out[me]

            return carry

        lax.fori_loop(0, per, give_back, 0)

    for k in range(CHUNKS):
        run(k)
        if k > 0:
            add_cores(k - 1)
        if k > 1:
            add_chips(k - 2)
    add_cores(CHUNKS - 1)
    if CHUNKS > 1:
        add_chips(CHUNKS - 2)

    for i in range(n_expert):
        sync_f[i * block : (i + 1) * block, :] = dn_in[i].astype(F32)[:block]
    sync_ref[...] = sync_f[...].astype(BF)
    add_chips(CHUNKS - 1)

    drain(ret_in.at[pl.ds(0, n_expert - 1)], sem.at[RET_R])
    returned = ret_in[...].astype(F32).reshape(experts, 2, ROWS, wide)
    returned = (returned[:, 0] + returned[:, 1]).reshape(slots, wide)
    mix = dot(combine, returned, ((0,), (0,)), precision=EXACT)
    mix = dot(mix, stretch.astype(F32), ((1,), (1,)), precision=EXACT)
    out_ref[...] = (hidden + mix).astype(BF).reshape(STEPS, seqs, share)

    drain(gu_in.at[pl.ds(0, n_expert - 1)], sem.at[GU_S])
    drain(dn_in.at[pl.ds(0, n_expert - 1)], sem.at[DN_S])
    drain(part_in.at[pl.ds(0, n_head - 1)], sem.at[PART_S])
    drain(tok_all.at[0, pl.ds(0, n_expert - 1)], sem.at[TOK_S])
    drain(ret_in.at[pl.ds(0, n_expert - 1)], sem.at[RET_S])
    drain(tok_all.at[pl.ds(0, n_head - 1)], sem.at[AG_S])
    drain(y_in, sem.at[Y_S])
    drain(z_in, sem.at[Z_S])


def local(
    n_expert,
    n_head,
    queries,
    cache_band,
    new_kv,
    cache_lengths,
    sink_logits,
    o_weight,
    residual,
    norm_gain,
    route_logits,
    routes,
    old_experts,
    new_experts,
    train_gate_up,
    train_down,
):
    experts = old_experts.shape[0]
    seqs = queries.shape[1]
    cols = STEPS * seqs
    block = train_gate_up.shape[1]
    padded = -(-block // 16) * 16
    share = residual.shape[2]
    wide = n_expert // n_head * padded
    half = train_gate_up.shape[3] // 2
    n_chip = n_head // 2
    width = norm_gain.shape[0]
    counter = jnp.arange(experts, dtype=jnp.int32)
    position = jnp.sum(
        jnp.where(old_experts[None, :] == new_experts[:, None], counter[None, :], 0), axis=1
    )
    logits = jnp.transpose(route_logits, (2, 0, 1)).reshape(TOP, cols)
    choices = jnp.transpose(routes, (2, 0, 1)).reshape(TOP, cols)
    vmem = pl.BlockSpec(memory_space=pltpu.VMEM)
    out, synced = pl.pallas_call(
        functools.partial(kernel, n_expert, n_head),
        out_shape=(
            jax.ShapeDtypeStruct((STEPS, seqs, share), BF),
            jax.ShapeDtypeStruct((width, half), BF),
        ),
        in_specs=[pl.BlockSpec(memory_space=pltpu.SMEM)] + [vmem] * 13,
        out_specs=(vmem, vmem),
        scratch_shapes=[
            pltpu.VMEM((2, block * experts, half), F32),
            pltpu.VMEM((experts, 2, padded, 2 * half), BF),
            pltpu.VMEM((experts, 2, padded, half), BF),
            pltpu.VMEM((n_expert, padded, 2 * half), BF),
            pltpu.VMEM((n_expert, padded, half), BF),
            pltpu.VMEM((n_head, cols, share), BF),
            pltpu.VMEM((n_head, cols, share), BF),
            pltpu.VMEM((experts, ROWS, wide), BF),
            pltpu.VMEM((n_head, n_expert, ROWS, wide), BF),
            pltpu.VMEM((n_chip, 2, n_expert, ROWS, wide), BF),
            pltpu.VMEM((n_chip, n_expert, ROWS, wide), BF),
            pltpu.VMEM((n_chip, n_expert, ROWS, wide), BF),
            pltpu.VMEM((n_chip - 1, n_expert, ROWS, wide), BF),
            pltpu.VMEM((n_expert, ROWS, wide), BF),
            pltpu.VMEM((n_expert, ROWS, wide), BF),
            pltpu.VMEM((width, half), F32),
            pltpu.SemaphoreType.DMA((13,)),
            pltpu.SemaphoreType.DMA((CHUNKS, n_head)),
            pltpu.SemaphoreType.DMA((CHUNKS, n_chip)),
        ],
        compiler_params=pltpu.CompilerParams(
            collective_id=0, has_side_effects=True, vmem_limit_bytes=56 << 20
        ),
    )(
        position,
        new_experts.reshape(1, -1),
        cache_lengths.reshape(1, -1),
        sink_logits.reshape(1, -1),
        logits,
        choices,
        norm_gain.reshape(n_head, share),
        queries,
        cache_band,
        new_kv,
        o_weight.T,
        residual,
        train_gate_up,
        jnp.transpose(train_down, (1, 0, 2)),
    )
    return out, synced[None]


def solution(mesh):
    in_specs = (
        P(None, "expert", "head"),
        P("expert", None, "head"),
        P(None, "expert", "head"),
        P("expert"),
        P("head"),
        P("head", None),
        P(None, "expert", "head"),
        P(),
        P(None, "expert", None),
        P(None, "expert", None),
        P(),
        P(),
        P(None, "expert", None, "head"),
        P(None, "expert", "head"),
    )
    out_specs = (P(None, "expert", "head"), P("expert", None, "head"))
    body = functools.partial(local, mesh.shape["expert"], mesh.shape["head"])
    return jax.shard_map(body, mesh=mesh, in_specs=in_specs, out_specs=out_specs, check_vma=False)
```

```python
import functools
import jax
import jax.numpy as jnp
from jax import lax
from jax.experimental import pallas as pl
from jax.experimental.pallas import tpu as pltpu
from jax.sharding import PartitionSpec as P

HD = 64
TOP = 4
STEPS = 2
GROUP = 4
CAP = 8
ROWS = STEPS * CAP
EPSILON = 1e-05
CHUNKS = 4
STRIDE = 11
FIRST_BATCH = 12
DOWN_EARLY = 16
MESH = pl.DeviceIdType.MESH
BF = jnp.bfloat16
F32 = jnp.float32
EXACT = lax.Precision.HIGHEST


def iota(shape, dim):
    return lax.broadcasted_iota(jnp.int32, shape, dim)


def dot(a, b, dims=((1,), (0,)), precision=None):
    return lax.dot_general(a, b, (dims, ((), ())), preferred_element_type=F32, precision=precision)


def column(row, size):
    eye = iota((size, size), 0) == iota((size, size), 1)
    return jnp.sum(jnp.where(eye, row, 0.0), axis=1, keepdims=True)


def log2(n):
    assert n & (n - 1) == 0
    return n.bit_length() - 1


def kernel(
    n_expert,
    n_head,
    pos_ref,
    new_ref,
    len_ref,
    sink_ref,
    logit_ref,
    route_ref,
    gain_ref,
    query_ref,
    band_ref,
    new_kv_ref,
    o_ref,
    residual_ref,
    gate_up_ref,
    down_ref,
    out_ref,
    sync_ref,
    down_f,
    gu_out,
    dn_out,
    gu_in,
    dn_in,
    part_out,
    part_in,
    square_out,
    square_in,
    tok_out,
    tok_all,
    half_f,
    half_out,
    half_in,
    act_all,
    y_out,
    y_in,
    z_out,
    z_in,
    ret_out,
    ret_in,
    sync_in,
    sync_f,
    sem,
    tok_sem,
    ag_sem,
    pair_sem,
    rs_sem,
):
    experts = n_expert // 2
    n_chip = n_head // 2
    seqs = query_ref.shape[1]
    cols = STEPS * seqs
    block = gate_up_ref.shape[1]
    padded = gu_in.shape[1]
    share = residual_ref.shape[2]
    per_head = n_expert // n_head
    wide = per_head * padded
    width = n_head * share
    units = gate_up_ref.shape[3]
    half = units // 2
    seq_bits = log2(seqs)
    per = n_expert // CHUNKS

    me = lax.axis_index("expert")
    head = lax.axis_index("head")
    core = lax.rem(head, 2)
    chip = head // 2
    mate = head + 1 - 2 * core
    my_slot = me // 2
    my_side = lax.rem(me, 2)
    partner = me + 1 - 2 * my_side
    row_head = me // per_head
    row_side = lax.rem(row_head, 2)
    row_index = (row_head // 2) * per_head + lax.rem(me, per_head)
    my_chunk = lax.rem(me + me // (2 * CHUNKS), CHUNKS)
    my_spot = my_chunk * per + me // CHUNKS
    gathers = my_side == core
    keeps_rows = my_side == row_side

    barrier = pltpu.get_barrier_semaphore()

    def greet_expert(i, carry):
        pl.semaphore_signal(
            barrier, inc=1, device_id=(lax.rem(me + i, n_expert), head), device_id_type=MESH
        )
        return carry

    def greet_head(i, carry):
        pl.semaphore_signal(
            barrier, inc=1, device_id=(me, lax.rem(head + i, n_head)), device_id_type=MESH
        )
        return carry

    lax.fori_loop(1, n_expert, greet_expert, 0)
    lax.fori_loop(1, n_head, greet_head, 0)

    for p in range(2):
        down_f[p] = (
            down_ref[:, :, p * half : (p + 1) * half].astype(F32).reshape(block * experts, half)
        )
    pad = padded - block
    last = padded - 16
    gu_out[:, last:, :] = jnp.zeros((experts, 16, 2 * units), BF)
    dn_out[:, last:, :] = jnp.zeros((experts, 16, units), BF)

    GU_S, GU_R, DN_S, DN_R, PART_S, PART_R, SQ_S, SQ_R = range(8)
    TOK_S, AG_S, HALF_S, ACT_S, Y_S, Z_S, RET_S, RET_R, SYNC_S, SYNC_R = range(8, 18)

    def send(src, dst, e, h, s, r):
        pltpu.make_async_remote_copy(
            src_ref=src,
            dst_ref=dst,
            send_sem=s,
            recv_sem=r,
            device_id=(e, h),
            device_id_type=MESH,
        ).start()

    def drain(ref, s):
        pltpu.make_async_copy(ref, ref, s).wait()

    def prepare_gate_up(slot):
        index = pos_ref[slot]
        for c in range(2):
            gu_out[slot, :block, c * units : (c + 1) * units] = gate_up_ref[index, :, c, :]

    def prepare_down(slot):
        index = pos_ref[slot]
        for p in range(2):
            dn_out[slot, :block, p * half : (p + 1) * half] = down_f[
                p, pl.ds(index, block, stride=experts), :
            ].astype(BF)

    def order(i):
        step = lax.rem(i * STRIDE, experts)
        return lax.rem(my_slot + jnp.where(core == 0, step, experts - step), experts)

    def send_gate_up(i, carry):
        slot = order(i)
        prepare_gate_up(slot)
        to = 2 * slot + row_side
        send(gu_out.at[slot], gu_in.at[row_index], to, head, sem.at[GU_S], sem.at[GU_R])
        return carry

    def send_down(i, carry):
        slot = order(i)
        prepare_down(slot)
        to = 2 * slot + row_side
        send(dn_out.at[slot], dn_in.at[row_index], to, head, sem.at[DN_S], sem.at[DN_R])
        return carry

    lanes = 2 * HD
    rows = STEPS * GROUP * seqs
    r_id = iota((rows, cols), 0)
    c_id = iota((rows, cols), 1)
    same = ((r_id >> 3) == (c_id & (seqs - 1))) & (((r_id >> 2) & 1) == (c_id >> seq_bits))
    rt_id = iota((cols, rows), 1)
    ct_id = iota((cols, rows), 0)
    same_t = ((rt_id >> 3) == (ct_id & (seqs - 1))) & (((rt_id >> 2) & 1) == (ct_id >> seq_bits))
    flat_q = query_ref[...].reshape(cols, GROUP * HD)
    spread_q = jnp.zeros((rows, lanes), F32)
    for g in range(GROUP):
        k_id = iota((GROUP * HD, lanes), 0)
        l_id = iota((GROUP * HD, lanes), 1)
        pick = ((k_id == g * HD + l_id) & (l_id < HD)).astype(BF)
        part = dot(flat_q, pick).astype(BF)
        spread_q += dot((same & ((r_id & 3) == g)).astype(BF), part)
    repeat = ((iota((rows, seqs), 0) >> 3) == iota((rows, seqs), 1)).astype(BF)
    fresh = [dot(repeat, new_kv_ref[s]) for s in range(STEPS)]
    row_s = (iota((rows, 1), 0) >> 2) & 1
    row_g = iota((rows, 1), 0) & 3
    lengths = jnp.sum(
        jnp.where(
            (iota((rows, seqs), 0) >> 3) == iota((rows, seqs), 1), len_ref[...].astype(F32), 0.0
        ),
        axis=1,
        keepdims=True,
    )
    sink = jnp.sum(
        jnp.where(row_g == iota((rows, GROUP), 1), sink_ref[...], 0.0), axis=1, keepdims=True
    )
    scale = HD**-0.5
    batched = (((2,), (2,)), ((0,), (0,)))
    scores = (
        lax.dot_general(
            spread_q.reshape(seqs, STEPS * GROUP, lanes).astype(BF),
            band_ref[...],
            batched,
            preferred_element_type=F32,
        ).reshape(rows, -1)
        * scale
    )
    window = band_ref.shape[1]
    w_id = iota((rows, window), 1)
    kept = (w_id >= row_s + 1) & (w_id.astype(F32) >= window - lengths)
    scores = jnp.where(kept, scores, -1e30)
    new_scores = [
        jnp.sum(spread_q * fresh[s], axis=1, keepdims=True) * scale for s in range(STEPS)
    ]
    new_scores[1] = jnp.where(row_s == 1, new_scores[1], -1e30)
    top = jnp.maximum(jnp.max(scores, axis=1, keepdims=True), sink)
    top = jnp.maximum(jnp.maximum(top, new_scores[0]), new_scores[1])
    raised = jnp.exp(scores - top)
    new_raised = [jnp.exp(n - top) for n in new_scores]
    total = jnp.sum(raised, axis=1, keepdims=True) + jnp.exp(sink - top)
    total = total + new_raised[0] + new_raised[1]
    probs = (raised / total).reshape(seqs, STEPS * GROUP, window).astype(BF)
    mixed = lax.dot_general(
        probs, band_ref[...], (((2,), (1,)), ((0,), (0,))), preferred_element_type=F32
    ).reshape(rows, lanes)
    for s in range(STEPS):
        mixed += (new_raised[s] / total).astype(BF).astype(F32) * fresh[s]
    mixed = mixed.astype(BF)
    attended = jnp.zeros((cols, GROUP * HD), F32)
    for g in range(GROUP):
        l_id = iota((lanes, GROUP * HD), 0)
        k_id = iota((lanes, GROUP * HD), 1)
        pick = ((k_id - g * HD == l_id - HD) & (l_id >= HD)).astype(BF)
        part = dot(mixed, pick).astype(BF)
        attended += dot((same_t & ((rt_id & 3) == g)).astype(BF), part)
    attended = attended.astype(BF)

    for j in range(n_head):
        part_out[j] = dot(attended, o_ref[j * share : (j + 1) * share, :], ((1,), (1,))).astype(BF)

    pl.semaphore_wait(barrier, n_expert + n_head - 2)

    def send_part(i, carry):
        to = lax.rem(head + i, n_head)
        send(part_out.at[to], part_in.at[head], me, to, sem.at[PART_S], sem.at[PART_R])
        return carry

    lax.fori_loop(1, n_head, send_part, 0)
    part_in[head] = part_out[head]

    prepare_gate_up(my_slot)
    prepare_down(my_slot)

    @pl.when(keeps_rows)
    def _():
        pltpu.make_async_copy(gu_out.at[my_slot], gu_in.at[row_index], sem.at[GU_R]).start()
        pltpu.make_async_copy(dn_out.at[my_slot], dn_in.at[row_index], sem.at[DN_R]).start()

    @pl.when(jnp.logical_not(keeps_rows))
    def _():
        send(
            gu_out.at[my_slot], gu_in.at[row_index], partner, head, sem.at[GU_S], sem.at[GU_R]
        )
        send(
            dn_out.at[my_slot], dn_in.at[row_index], partner, head, sem.at[DN_S], sem.at[DN_R]
        )

    lax.fori_loop(1, FIRST_BATCH, send_gate_up, 0)

    new_col = column(new_ref[...].astype(F32), experts)
    logits = [logit_ref[j : j + 1, :] for j in range(TOP)]
    highest = functools.reduce(jnp.maximum, logits)
    powers = [jnp.exp(l - highest) for l in logits]
    power_sum = functools.reduce(jnp.add, powers)
    member = jnp.zeros((experts, cols), F32)
    weight = jnp.zeros((experts, cols), F32)
    for j in range(TOP):
        hit = (route_ref[j : j + 1, :].astype(F32) == new_col).astype(F32)
        member += hit
        weight += hit * (powers[j] / power_sum)
    u0 = iota((cols, cols), 0)
    u1 = iota((cols, cols), 1)
    before = ((u0 < u1) & ((u0 >> seq_bits) == (u1 >> seq_bits))).astype(BF)
    rank = dot(member.astype(BF), before)
    slots = experts * ROWS
    of_slot = ((iota((slots, experts), 0) >> 4) == iota((slots, experts), 1)).astype(BF)
    member_rows = dot(of_slot, member.astype(BF))
    rank_rows = dot(of_slot, rank.astype(BF))
    i_id = iota((slots, cols), 0)
    place = (
        member_rows
        * (rank_rows == (i_id & 7).astype(F32)).astype(F32)
        * (((i_id >> 3) & 1) == (iota((slots, cols), 1) >> seq_bits)).astype(F32)
    )
    combine = dot(of_slot.astype(F32), weight, precision=EXACT) * place

    drain(part_in.at[pl.ds(0, n_head - 1)], sem.at[PART_R])
    hidden = residual_ref[...].reshape(cols, share).astype(F32)
    for j in range(n_head):
        hidden += part_in[j].astype(F32)
    squares = jnp.sum(hidden * hidden, axis=1, keepdims=True)
    square_row = jnp.sum(
        jnp.where(iota((cols, cols), 0) == iota((cols, cols), 1), squares, 0.0),
        axis=0,
        keepdims=True,
    )
    square_out[...] = jnp.broadcast_to(square_row, square_out.shape)

    def send_square(i, carry):
        to = lax.rem(head + i, n_head)
        send(square_out, square_in.at[head], me, to, sem.at[SQ_S], sem.at[SQ_R])
        return carry

    lax.fori_loop(1, n_head, send_square, 0)
    square_in[head] = square_out[...]
    lane = iota((share, wide), 1)
    gap = jnp.zeros((share, wide), jnp.int32)
    for b in range(1, per_head):
        gap += pad * (iota((share, wide), 0) >= b * block).astype(jnp.int32)
    stretch = (iota((share, wide), 0) + gap == lane).astype(BF)
    gained = hidden * gain_ref[pl.ds(head, 1), :]
    drain(square_in.at[pl.ds(0, n_head - 1)], sem.at[SQ_R])
    all_squares = jnp.zeros((1, cols), F32)
    for j in range(n_head):
        all_squares += square_in[j, 0:1, :]
    norm = column(lax.rsqrt(all_squares * (1.0 / width) + EPSILON), cols)
    token = dot((gained * norm).astype(BF), stretch).astype(BF)
    tok_out[...] = dot(place.astype(BF), token).astype(BF).reshape(experts, ROWS, wide)

    def send_token(i, carry):
        slot = order(i)
        send(
            tok_out.at[slot],
            tok_all.at[chip, my_spot],
            2 * slot + core,
            head,
            sem.at[TOK_S],
            tok_sem.at[my_chunk],
        )
        return carry

    @pl.when(gathers)
    def _():
        pltpu.make_async_copy(
            tok_out.at[my_slot], tok_all.at[chip, my_spot], tok_sem.at[my_chunk]
        ).start()

    @pl.when(jnp.logical_not(gathers))
    def _():
        send(
            tok_out.at[my_slot],
            tok_all.at[chip, my_spot],
            partner,
            head,
            sem.at[TOK_S],
            tok_sem.at[my_chunk],
        )

    lax.fori_loop(1, experts, send_token, 0)

    def feed(sent, count, limit):
        while count and sent[0] < experts:
            n = min(count, experts - sent[0])
            lax.fori_loop(sent[0], sent[0] + n, send_gate_up, 0)
            sent[0] += n
            count -= n
        n = min(count, limit - sent[1])
        if n > 0:
            lax.fori_loop(sent[1], sent[1] + n, send_down, 0)
            sent[1] += n

    def chunk(k):
        return pl.ds(k * per, per)

    @pl.when(gathers)
    def _():
        sent = [FIRST_BATCH, 1]
        feed(sent, 8, DOWN_EARLY)
        for k in range(CHUNKS):
            view = tok_all.at[chip, chunk(k)]
            drain(view, tok_sem.at[k])
            for d in range(1, n_chip):
                to = 2 * lax.rem(chip + d, n_chip) + core
                send(view, view, me, to, sem.at[AG_S], ag_sem.at[k, chip])
            send(view, view, me, mate, sem.at[AG_S], ag_sem.at[k, chip])
            feed(sent, 2, DOWN_EARLY)
        for k in range(CHUNKS):
            for d in range(1, n_chip):
                source = lax.rem(chip + n_chip - d, n_chip)
                view = tok_all.at[source, chunk(k)]
                drain(view, ag_sem.at[k, source])
                send(view, view, me, mate, sem.at[AG_S], ag_sem.at[k, source])
            feed(sent, 5, DOWN_EARLY)
        feed(sent, 2 * experts, DOWN_EARLY)

    @pl.when(jnp.logical_not(gathers))
    def _():
        feed([FIRST_BATCH, 1], 2 * experts, DOWN_EARLY)
        for k in range(CHUNKS):
            for source in range(n_chip):
                drain(tok_all.at[source, chunk(k)], ag_sem.at[k, source])

    drain(gu_in, sem.at[GU_R])
    size = per * ROWS
    part_size = size // 2
    sent = [experts, DOWN_EARLY]
    for k in range(CHUNKS):
        acc = jnp.zeros((size, 2 * units), F32)
        for j in range(0, n_chip, 2):
            rows_in = jnp.concatenate(
                [tok_all[j + i, chunk(k)].reshape(size, wide) for i in range(2)], axis=1
            )
            weights = gu_in[per_head * j : per_head * (j + 2)].reshape(2 * wide, 2 * units)
            acc += dot(rows_in, weights)
        for p in range(2):
            piece = acc[p * part_size : (p + 1) * part_size]
            half_f[k, p] = piece
            half_out[k, p] = piece.astype(BF)
        send(
            half_out.at[k, 1 - my_side],
            half_in.at[k],
            partner,
            head,
            sem.at[HALF_S],
            pair_sem.at[k, 0],
        )
        feed(sent, experts // CHUNKS, experts)
    feed(sent, experts, experts)
    for k in range(CHUNKS):
        drain(half_in.at[k], pair_sem.at[k, 0])
        acc = half_f[k, my_side] + half_in[k].astype(F32)
        gate = jnp.minimum(acc[:, :units], 7.0)
        up = jnp.clip(acc[:, units:], -7.0, 7.0)
        active = (up + 1.0) * gate * jax.nn.sigmoid(1.702 * gate)
        act_all[my_side, k] = active.astype(BF)
        view = act_all.at[my_side, k]
        send(view, view, partner, head, sem.at[ACT_S], pair_sem.at[k, 1])

    drain(dn_in, sem.at[DN_R])
    lanes_out = pl.ds(pl.multiple_of((1 - my_side) * half, half), half)
    lanes_own = pl.ds(pl.multiple_of(my_side * half, half), half)

    def run(k):
        drain(act_all.at[1 - my_side, k], pair_sem.at[k, 1])
        active = jnp.concatenate([act_all[0, k], act_all[1, k]], axis=0)
        for j in range(n_chip):
            weights = dn_in[per_head * j : per_head * (j + 1)].reshape(wide, units)
            y = dot(active, weights, ((1,), (1,))).astype(BF)
            y_out[j, chunk(k)] = y.reshape(per, ROWS, wide)

        @pl.when(jnp.logical_not(gathers))
        def _():
            send(
                y_out.at[:, chunk(k)],
                y_in.at[:, chunk(k)],
                me,
                mate,
                sem.at[Y_S],
                rs_sem.at[k, 0],
            )

    def add_cores(k):
        drain(y_in.at[:, chunk(k)], rs_sem.at[k, 0])
        for d in range(n_chip):
            to = lax.rem(chip + d, n_chip)
            z = y_out[to, chunk(k)].astype(F32) + y_in[to, chunk(k)].astype(F32)
            z_out[to, chunk(k)] = z.astype(BF)
            if d > 0:
                send(
                    z_out.at[to, chunk(k)],
                    z_in.at[d - 1, chunk(k)],
                    me,
                    2 * to + core,
                    sem.at[Z_S],
                    rs_sem.at[k, d],
                )

    def add_chips(k):
        total = z_out[chip, chunk(k)].astype(F32)
        for d in range(1, n_chip):
            drain(z_in.at[d - 1, chunk(k)], rs_sem.at[k, d])
            total += z_in[d - 1, chunk(k)].astype(F32)
        ret_out[chunk(k)] = total.astype(BF)

        def give_back(i, carry):
            m = lax.rem(me + 5 * i, per)
            to = CHUNKS * m + lax.rem(k + n_expert - m // 2, CHUNKS)
            row = ret_out.at[k * per + m]

            @pl.when(to != me)
            def _():
                send(row, ret_in.at[my_slot], to, head, sem.at[RET_S], sem.at[RET_R])

            @pl.when(to == me)
            def _():
                pltpu.make_async_copy(row, ret_in.at[my_slot], sem.at[RET_R]).start()

            return carry

        lax.fori_loop(0, per, give_back, 0)

    for k in range(CHUNKS):
        run(k)

        @pl.when(gathers)
        def _():
            if k > 0:
                add_cores(k - 1)
            if k > 1:
                add_chips(k - 2)

    @pl.when(gathers)
    def _():
        add_cores(CHUNKS - 1)
        add_chips(CHUNKS - 2)

    send(
        dn_in.at[:, :, lanes_out],
        sync_in.at[my_side],
        partner,
        head,
        sem.at[SYNC_S],
        sem.at[SYNC_R],
    )
    sync_in[my_side] = dn_in[:, :, lanes_own]

    @pl.when(gathers)
    def _():
        add_chips(CHUNKS - 1)

    drain(sync_in.at[1 - my_side], sem.at[SYNC_R])
    for i in range(n_expert):
        h, r = divmod(i, per_head)
        served = sync_in[h % 2, (h // 2) * per_head + r]
        sync_f[i * block : (i + 1) * block, :] = served.astype(F32)[:block]
    sync_ref[...] = sync_f[...].astype(BF)

    drain(ret_in, sem.at[RET_R])
    returned = ret_in[...].astype(F32).reshape(slots, wide)
    mix = dot(combine, returned, ((0,), (0,)), precision=EXACT)
    mix = dot(mix, stretch.astype(F32), ((1,), (1,)), precision=EXACT)
    out_ref[...] = (hidden + mix).astype(BF).reshape(STEPS, seqs, share)

    others = pl.ds(0, experts - 1)

    @pl.when(keeps_rows)
    def _():
        drain(gu_in.at[others], sem.at[GU_S])
        drain(dn_in.at[others], sem.at[DN_S])

    @pl.when(jnp.logical_not(keeps_rows))
    def _():
        drain(gu_in, sem.at[GU_S])
        drain(dn_in, sem.at[DN_S])

    drain(part_in.at[pl.ds(0, n_head - 1)], sem.at[PART_S])
    drain(square_in.at[pl.ds(0, n_head - 1)], sem.at[SQ_S])
    drain(half_in, sem.at[HALF_S])
    drain(act_all.at[0], sem.at[ACT_S])
    drain(sync_in.at[0], sem.at[SYNC_S])

    @pl.when(gathers)
    def _():
        drain(tok_out.at[others], sem.at[TOK_S])
        drain(tok_all, sem.at[AG_S])
        drain(tok_all.at[pl.ds(0, n_chip - 1)], sem.at[AG_S])
        drain(z_in, sem.at[Z_S])
        drain(ret_out.at[pl.ds(0, n_expert - 1)], sem.at[RET_S])

    @pl.when(jnp.logical_not(gathers))
    def _():
        drain(tok_out, sem.at[TOK_S])
        drain(y_in, sem.at[Y_S])


def local(
    n_expert,
    n_head,
    queries,
    cache_band,
    new_kv,
    cache_lengths,
    sink_logits,
    o_weight,
    residual,
    norm_gain,
    route_logits,
    routes,
    old_experts,
    new_experts,
    train_gate_up,
    train_down,
):
    experts = old_experts.shape[0]
    seqs = queries.shape[1]
    cols = STEPS * seqs
    block = train_gate_up.shape[1]
    padded = -(-block // 16) * 16
    share = residual.shape[2]
    wide = n_expert // n_head * padded
    units = train_gate_up.shape[3]
    half = units // 2
    size = n_expert // CHUNKS * ROWS
    n_chip = n_head // 2
    width = norm_gain.shape[0]
    counter = jnp.arange(experts, dtype=jnp.int32)
    position = jnp.sum(
        jnp.where(old_experts[None, :] == new_experts[:, None], counter[None, :], 0), axis=1
    )
    logits = jnp.transpose(route_logits, (2, 0, 1)).reshape(TOP, cols)
    choices = jnp.transpose(routes, (2, 0, 1)).reshape(TOP, cols)
    vmem = pl.BlockSpec(memory_space=pltpu.VMEM)
    out, synced = pl.pallas_call(
        functools.partial(kernel, n_expert, n_head),
        out_shape=(
            jax.ShapeDtypeStruct((STEPS, seqs, share), BF),
            jax.ShapeDtypeStruct((width, half), BF),
        ),
        in_specs=[pl.BlockSpec(memory_space=pltpu.SMEM)] + [vmem] * 13,
        out_specs=(vmem, vmem),
        scratch_shapes=[
            pltpu.VMEM((2, block * experts, half), F32),
            pltpu.VMEM((experts, padded, 2 * units), BF),
            pltpu.VMEM((experts, padded, units), BF),
            pltpu.VMEM((experts, padded, 2 * units), BF),
            pltpu.VMEM((experts, padded, units), BF),
            pltpu.VMEM((n_head, cols, share), BF),
            pltpu.VMEM((n_head, cols, share), BF),
            pltpu.VMEM((8, cols), F32),
            pltpu.VMEM((n_head, 8, cols), F32),
            pltpu.VMEM((experts, ROWS, wide), BF),
            pltpu.VMEM((n_chip, n_expert, ROWS, wide), BF),
            pltpu.VMEM((CHUNKS, 2, size // 2, 2 * units), F32),
            pltpu.VMEM((CHUNKS, 2, size // 2, 2 * units), BF),
            pltpu.VMEM((CHUNKS, size // 2, 2 * units), BF),
            pltpu.VMEM((2, CHUNKS, size // 2, units), BF),
            pltpu.VMEM((n_chip, n_expert, ROWS, wide), BF),
            pltpu.VMEM((n_chip, n_expert, ROWS, wide), BF),
            pltpu.VMEM((n_chip, n_expert, ROWS, wide), BF),
            pltpu.VMEM((n_chip - 1, n_expert, ROWS, wide), BF),
            pltpu.VMEM((n_expert, ROWS, wide), BF),
            pltpu.VMEM((experts, ROWS, wide), BF),
            pltpu.VMEM((2, experts, padded, half), BF),
            pltpu.VMEM((width, half), F32),
            pltpu.SemaphoreType.DMA((18,)),
            pltpu.SemaphoreType.DMA((CHUNKS,)),
            pltpu.SemaphoreType.DMA((CHUNKS, n_chip)),
            pltpu.SemaphoreType.DMA((CHUNKS, 2)),
            pltpu.SemaphoreType.DMA((CHUNKS, n_chip)),
        ],
        compiler_params=pltpu.CompilerParams(
            collective_id=0, has_side_effects=True, vmem_limit_bytes=56 << 20
        ),
    )(
        position,
        new_experts.reshape(1, -1),
        cache_lengths.reshape(1, -1),
        sink_logits.reshape(1, -1),
        logits,
        choices,
        norm_gain.reshape(n_head, share),
        queries,
        cache_band,
        new_kv,
        o_weight.T,
        residual,
        train_gate_up,
        jnp.transpose(train_down, (1, 0, 2)),
    )
    return out, synced[None]


def solution(mesh):
    in_specs = (
        P(None, "expert", "head"),
        P("expert", None, "head"),
        P(None, "expert", "head"),
        P("expert"),
        P("head"),
        P("head", None),
        P(None, "expert", "head"),
        P(),
        P(None, "expert", None),
        P(None, "expert", None),
        P(),
        P(),
        P(None, "expert", None, "head"),
        P(None, "expert", "head"),
    )
    out_specs = (P(None, "expert", "head"), P("expert", None, "head"))
    body = functools.partial(local, mesh.shape["expert"], mesh.shape["head"])
    return jax.shard_map(body, mesh=mesh, in_specs=in_specs, out_specs=out_specs, check_vma=False)
```

```python
import functools
import jax
import jax.numpy as jnp
from jax import lax
from jax.experimental import pallas as pl
from jax.experimental.pallas import tpu as pltpu
from jax.sharding import PartitionSpec as P

HD = 64
TOP = 4
STEPS = 2
GROUP = 4
CAP = 8
ROWS = STEPS * CAP
EPSILON = 1e-05
CHUNKS = 4
STRIDE = 11
FIRST_BATCH = 6
DOWN_EARLY = 16
MESH = pl.DeviceIdType.MESH
BF = jnp.bfloat16
F32 = jnp.float32
EXACT = lax.Precision.HIGHEST


def iota(shape, dim):
    return lax.broadcasted_iota(jnp.int32, shape, dim)


def dot(a, b, dims=((1,), (0,)), precision=None):
    return lax.dot_general(a, b, (dims, ((), ())), preferred_element_type=F32, precision=precision)


def column(row, size):
    eye = iota((size, size), 0) == iota((size, size), 1)
    return jnp.sum(jnp.where(eye, row, 0.0), axis=1, keepdims=True)


def log2(n):
    assert n & (n - 1) == 0
    return n.bit_length() - 1


def kernel(
    n_expert,
    n_head,
    old_slot_ref,
    new_slot_ref,
    new_ref,
    len_ref,
    sink_ref,
    logit_ref,
    route_ref,
    gain_ref,
    query_ref,
    band_ref,
    new_kv_ref,
    o_ref,
    residual_ref,
    gate_up_ref,
    down_ref,
    out_ref,
    sync_ref,
    down_f,
    gu_out,
    dn_out,
    gu_in,
    dn_in,
    part_out,
    part_in,
    square_out,
    square_in,
    tok_out,
    tok_all,
    half_f,
    half_out,
    half_in,
    act_all,
    y_out,
    y_in,
    z_out,
    z_in,
    ret_out,
    ret_in,
    sync_in,
    sync_f,
    logit_all,
    route_all,
    sem,
    tok_sem,
    ag_sem,
    pair_sem,
    rs_sem,
):
    experts = n_expert // 2
    n_chip = n_head // 2
    seqs = query_ref.shape[1]
    cols = STEPS * seqs
    block = gate_up_ref.shape[1]
    padded = gu_in.shape[1]
    share = residual_ref.shape[2]
    per_head = n_expert // n_head
    wide = per_head * padded
    width = n_head * share
    units = gate_up_ref.shape[3]
    half = units // 2
    seq_bits = log2(seqs)
    per = n_expert // CHUNKS

    me = lax.axis_index("expert")
    head = lax.axis_index("head")
    core = lax.rem(head, 2)
    chip = head // 2
    mate = head + 1 - 2 * core
    my_slot = me // 2
    my_side = lax.rem(me, 2)
    partner = me + 1 - 2 * my_side
    row_head = me // per_head
    row_side = lax.rem(row_head, 2)
    row_index = (row_head // 2) * per_head + lax.rem(me, per_head)
    my_chunk = lax.rem(me + me // (2 * CHUNKS), CHUNKS)
    my_spot = my_chunk * per + me // CHUNKS
    gathers = my_side == core
    keeps_rows = my_side == row_side

    barrier = pltpu.get_barrier_semaphore()

    def greet_expert(i, carry):
        pl.semaphore_signal(
            barrier, inc=1, device_id=(lax.rem(me + i, n_expert), head), device_id_type=MESH
        )
        return carry

    def greet_head(i, carry):
        pl.semaphore_signal(
            barrier, inc=1, device_id=(me, lax.rem(head + i, n_head)), device_id_type=MESH
        )
        return carry

    lax.fori_loop(1, n_expert, greet_expert, 0)
    lax.fori_loop(1, n_head, greet_head, 0)

    for p in range(2):
        down_f[p] = (
            down_ref[:, :, p * half : (p + 1) * half].astype(F32).reshape(block * experts, half)
        )
    pad = padded - block
    last = padded - 16
    gu_out[:, last:, :] = jnp.zeros((experts, 16, 2 * units), BF)
    dn_out[:, last:, :] = jnp.zeros((experts, 16, units), BF)

    GU_S, GU_R, DN_S, DN_R, PART_S, PART_R, SQ_S, SQ_R = range(8)
    TOK_S, AG_S, HALF_S, ACT_S, Y_S, Z_S, RET_S, RET_R, SYNC_S, SYNC_R = range(8, 18)

    def send(src, dst, e, h, s, r):
        pltpu.make_async_remote_copy(
            src_ref=src,
            dst_ref=dst,
            send_sem=s,
            recv_sem=r,
            device_id=(e, h),
            device_id_type=MESH,
        ).start()

    def drain(ref, s):
        pltpu.make_async_copy(ref, ref, s).wait()

    def position(slot):
        expert = new_slot_ref[slot]
        found = jnp.int32(0)
        for k in range(1, experts):
            found = jnp.where(old_slot_ref[k] == expert, k, found)
        return found

    def prepare_gate_up(slot):
        index = position(slot)
        for c in range(2):
            gu_out[slot, :block, c * units : (c + 1) * units] = gate_up_ref[index, :, c, :]

    def prepare_down(slot):
        index = position(slot)
        for p in range(2):
            dn_out[slot, :block, p * half : (p + 1) * half] = down_f[
                p, pl.ds(index, block, stride=experts), :
            ].astype(BF)

    def order(i):
        step = lax.rem(i * STRIDE, experts)
        return lax.rem(my_slot + jnp.where(core == 0, step, experts - step), experts)

    def send_gate_up(i, carry):
        slot = order(i)
        prepare_gate_up(slot)
        to = 2 * slot + row_side
        send(gu_out.at[slot], gu_in.at[row_index], to, head, sem.at[GU_S], sem.at[GU_R])
        return carry

    def send_down(i, carry):
        slot = order(i)
        prepare_down(slot)
        to = 2 * slot + row_side
        send(dn_out.at[slot], dn_in.at[row_index], to, head, sem.at[DN_S], sem.at[DN_R])
        return carry

    lanes = 2 * HD
    rows = STEPS * GROUP * seqs
    r_id = iota((rows, cols), 0)
    c_id = iota((rows, cols), 1)
    same = ((r_id >> 3) == (c_id & (seqs - 1))) & (((r_id >> 2) & 1) == (c_id >> seq_bits))
    rt_id = iota((cols, rows), 1)
    ct_id = iota((cols, rows), 0)
    same_t = ((rt_id >> 3) == (ct_id & (seqs - 1))) & (((rt_id >> 2) & 1) == (ct_id >> seq_bits))
    flat_q = query_ref[...].reshape(cols, GROUP * HD)
    spread_q = jnp.zeros((rows, lanes), F32)
    for g in range(GROUP):
        k_id = iota((GROUP * HD, lanes), 0)
        l_id = iota((GROUP * HD, lanes), 1)
        pick = ((k_id == g * HD + l_id) & (l_id < HD)).astype(BF)
        part = dot(flat_q, pick).astype(BF)
        spread_q += dot((same & ((r_id & 3) == g)).astype(BF), part)
    repeat = ((iota((rows, seqs), 0) >> 3) == iota((rows, seqs), 1)).astype(BF)
    fresh = [dot(repeat, new_kv_ref[s]) for s in range(STEPS)]
    row_s = (iota((rows, 1), 0) >> 2) & 1
    row_g = iota((rows, 1), 0) & 3
    lengths = jnp.sum(
        jnp.where(
            (iota((rows, seqs), 0) >> 3) == iota((rows, seqs), 1), len_ref[...].astype(F32), 0.0
        ),
        axis=1,
        keepdims=True,
    )
    sink = jnp.sum(
        jnp.where(row_g == iota((rows, GROUP), 1), sink_ref[...], 0.0), axis=1, keepdims=True
    )
    scale = HD**-0.5
    batched = (((2,), (2,)), ((0,), (0,)))
    scores = (
        lax.dot_general(
            spread_q.reshape(seqs, STEPS * GROUP, lanes).astype(BF),
            band_ref[...],
            batched,
            preferred_element_type=F32,
        ).reshape(rows, -1)
        * scale
    )
    window = band_ref.shape[1]
    w_id = iota((rows, window), 1)
    kept = (w_id >= row_s + 1) & (w_id.astype(F32) >= window - lengths)
    scores = jnp.where(kept, scores, -1e30)
    new_scores = [
        jnp.sum(spread_q * fresh[s], axis=1, keepdims=True) * scale for s in range(STEPS)
    ]
    new_scores[1] = jnp.where(row_s == 1, new_scores[1], -1e30)
    top = jnp.maximum(jnp.max(scores, axis=1, keepdims=True), sink)
    top = jnp.maximum(jnp.maximum(top, new_scores[0]), new_scores[1])
    raised = jnp.exp(scores - top)
    new_raised = [jnp.exp(n - top) for n in new_scores]
    total = jnp.sum(raised, axis=1, keepdims=True) + jnp.exp(sink - top)
    total = total + new_raised[0] + new_raised[1]
    probs = (raised / total).reshape(seqs, STEPS * GROUP, window).astype(BF)
    mixed = lax.dot_general(
        probs, band_ref[...], (((2,), (1,)), ((0,), (0,))), preferred_element_type=F32
    ).reshape(rows, lanes)
    for s in range(STEPS):
        mixed += (new_raised[s] / total).astype(BF).astype(F32) * fresh[s]
    mixed = mixed.astype(BF)
    attended = jnp.zeros((cols, GROUP * HD), F32)
    for g in range(GROUP):
        l_id = iota((lanes, GROUP * HD), 0)
        k_id = iota((lanes, GROUP * HD), 1)
        pick = ((k_id - g * HD == l_id - HD) & (l_id >= HD)).astype(BF)
        part = dot(mixed, pick).astype(BF)
        attended += dot((same_t & ((rt_id & 3) == g)).astype(BF), part)
    attended = attended.astype(BF)

    for j in range(n_head):
        part_out[j] = dot(attended, o_ref[j * share : (j + 1) * share, :], ((1,), (1,))).astype(BF)

    pl.semaphore_wait(barrier, n_expert + n_head - 2)

    def send_part(i, carry):
        to = lax.rem(head + i, n_head)
        send(part_out.at[to], part_in.at[head], me, to, sem.at[PART_S], sem.at[PART_R])
        return carry

    lax.fori_loop(1, n_head, send_part, 0)
    part_in[head] = part_out[head]

    prepare_gate_up(my_slot)
    prepare_down(my_slot)

    @pl.when(keeps_rows)
    def _():
        pltpu.make_async_copy(gu_out.at[my_slot], gu_in.at[row_index], sem.at[GU_R]).start()
        pltpu.make_async_copy(dn_out.at[my_slot], dn_in.at[row_index], sem.at[DN_R]).start()

    @pl.when(jnp.logical_not(keeps_rows))
    def _():
        send(
            gu_out.at[my_slot], gu_in.at[row_index], partner, head, sem.at[GU_S], sem.at[GU_R]
        )
        send(
            dn_out.at[my_slot], dn_in.at[row_index], partner, head, sem.at[DN_S], sem.at[DN_R]
        )

    lax.fori_loop(1, FIRST_BATCH, send_gate_up, 0)

    new_col = column(new_ref[...].astype(F32), experts)
    for s in range(STEPS):
        logit_all[:, s * seqs : (s + 1) * seqs] = logit_ref[s]
        route_all[:, s * seqs : (s + 1) * seqs] = route_ref[s].astype(F32)
    logits = [logit_all[j : j + 1, :] for j in range(TOP)]
    highest = functools.reduce(jnp.maximum, logits)
    powers = [jnp.exp(l - highest) for l in logits]
    power_sum = functools.reduce(jnp.add, powers)
    member = jnp.zeros((experts, cols), F32)
    weight = jnp.zeros((experts, cols), F32)
    for j in range(TOP):
        hit = (route_all[j : j + 1, :] == new_col).astype(F32)
        member += hit
        weight += hit * (powers[j] / power_sum)
    u0 = iota((cols, cols), 0)
    u1 = iota((cols, cols), 1)
    before = ((u0 < u1) & ((u0 >> seq_bits) == (u1 >> seq_bits))).astype(BF)
    rank = dot(member.astype(BF), before)
    slots = experts * ROWS
    of_slot = ((iota((slots, experts), 0) >> 4) == iota((slots, experts), 1)).astype(BF)
    member_rows = dot(of_slot, member.astype(BF))
    rank_rows = dot(of_slot, rank.astype(BF))
    i_id = iota((slots, cols), 0)
    place = (
        member_rows
        * (rank_rows == (i_id & 7).astype(F32)).astype(F32)
        * (((i_id >> 3) & 1) == (iota((slots, cols), 1) >> seq_bits)).astype(F32)
    )
    combine = dot(of_slot.astype(F32), weight, precision=EXACT) * place

    drain(part_in.at[pl.ds(0, n_head - 1)], sem.at[PART_R])
    hidden = residual_ref[...].reshape(cols, share).astype(F32)
    for j in range(n_head):
        hidden += part_in[j].astype(F32)
    squares = jnp.sum(hidden * hidden, axis=1, keepdims=True)
    square_row = jnp.sum(
        jnp.where(iota((cols, cols), 0) == iota((cols, cols), 1), squares, 0.0),
        axis=0,
        keepdims=True,
    )
    square_out[...] = jnp.broadcast_to(square_row, square_out.shape)

    def send_square(i, carry):
        to = lax.rem(head + i, n_head)
        send(square_out, square_in.at[head], me, to, sem.at[SQ_S], sem.at[SQ_R])
        return carry

    lax.fori_loop(1, n_head, send_square, 0)
    square_in[head] = square_out[...]
    lane = iota((share, wide), 1)
    gap = jnp.zeros((share, wide), jnp.int32)
    for b in range(1, per_head):
        gap += pad * (iota((share, wide), 0) >= b * block).astype(jnp.int32)
    stretch = (iota((share, wide), 0) + gap == lane).astype(BF)
    gain = jnp.zeros((1, share), F32)
    for j in range(n_head):
        gain += jnp.where(head == j, gain_ref[:, j * share : (j + 1) * share], 0.0)
    gained = hidden * gain
    drain(square_in.at[pl.ds(0, n_head - 1)], sem.at[SQ_R])
    all_squares = jnp.zeros((1, cols), F32)
    for j in range(n_head):
        all_squares += square_in[j, 0:1, :]
    norm = column(lax.rsqrt(all_squares * (1.0 / width) + EPSILON), cols)
    token = dot((gained * norm).astype(BF), stretch).astype(BF)
    tok_out[...] = dot(place.astype(BF), token).astype(BF).reshape(experts, ROWS, wide)

    def send_token(i, carry):
        slot = order(i)
        send(
            tok_out.at[slot],
            tok_all.at[chip, my_spot],
            2 * slot + core,
            head,
            sem.at[TOK_S],
            tok_sem.at[my_chunk],
        )
        return carry

    @pl.when(gathers)
    def _():
        pltpu.make_async_copy(
            tok_out.at[my_slot], tok_all.at[chip, my_spot], tok_sem.at[my_chunk]
        ).start()

    @pl.when(jnp.logical_not(gathers))
    def _():
        send(
            tok_out.at[my_slot],
            tok_all.at[chip, my_spot],
            partner,
            head,
            sem.at[TOK_S],
            tok_sem.at[my_chunk],
        )

    lax.fori_loop(1, experts, send_token, 0)

    def feed(sent, count, limit):
        while count and sent[0] < experts:
            n = min(count, experts - sent[0])
            lax.fori_loop(sent[0], sent[0] + n, send_gate_up, 0)
            sent[0] += n
            count -= n
        n = min(count, limit - sent[1])
        if n > 0:
            lax.fori_loop(sent[1], sent[1] + n, send_down, 0)
            sent[1] += n

    def chunk(k):
        return pl.ds(k * per, per)

    @pl.when(gathers)
    def _():
        sent = [FIRST_BATCH, 1]
        feed(sent, 8, DOWN_EARLY)
        for k in range(CHUNKS):
            view = tok_all.at[chip, chunk(k)]
            drain(view, tok_sem.at[k])
            for d in range(1, n_chip):
                to = 2 * lax.rem(chip + d, n_chip) + core
                send(view, view, me, to, sem.at[AG_S], ag_sem.at[k, chip])
            send(view, view, me, mate, sem.at[AG_S], ag_sem.at[k, chip])
            feed(sent, 2, DOWN_EARLY)
        for k in range(CHUNKS):
            for d in range(1, n_chip):
                source = lax.rem(chip + n_chip - d, n_chip)
                view = tok_all.at[source, chunk(k)]
                drain(view, ag_sem.at[k, source])
                send(view, view, me, mate, sem.at[AG_S], ag_sem.at[k, source])
            feed(sent, 5, DOWN_EARLY)
        feed(sent, 2 * experts, DOWN_EARLY)

    @pl.when(jnp.logical_not(gathers))
    def _():
        feed([FIRST_BATCH, 1], 2 * experts, DOWN_EARLY)
        for k in range(CHUNKS):
            for source in range(n_chip):
                drain(tok_all.at[source, chunk(k)], ag_sem.at[k, source])

    drain(gu_in, sem.at[GU_R])
    size = per * ROWS
    part_size = size // 2
    sent = [experts, DOWN_EARLY]
    lanes_out = pl.ds(pl.multiple_of((1 - my_side) * half, half), half)
    lanes_own = pl.ds(pl.multiple_of(my_side * half, half), half)

    def part_sums(k):
        acc = jnp.zeros((size, 2 * units), F32)
        for j in range(0, n_chip, 2):
            rows_in = jnp.concatenate(
                [tok_all[j + i, chunk(k)].reshape(size, wide) for i in range(2)], axis=1
            )
            weights = gu_in[per_head * j : per_head * (j + 2)].reshape(2 * wide, 2 * units)
            acc += dot(rows_in, weights)
        for p in range(2):
            piece = acc[p * part_size : (p + 1) * part_size]
            half_f[k, p] = piece
            half_out[k, p] = piece.astype(BF)
        send(
            half_out.at[k, 1 - my_side],
            half_in.at[k],
            partner,
            head,
            sem.at[HALF_S],
            pair_sem.at[k, 0],
        )
        feed(sent, experts // CHUNKS, experts)

    def activate(k):
        drain(half_in.at[k], pair_sem.at[k, 0])
        acc = half_f[k, my_side] + half_in[k].astype(F32)
        gate = jnp.minimum(acc[:, :units], 7.0)
        up = jnp.clip(acc[:, units:], -7.0, 7.0)
        active = (up + 1.0) * gate * jax.nn.sigmoid(1.702 * gate)
        act_all[my_side, k] = active.astype(BF)
        view = act_all.at[my_side, k]
        send(view, view, partner, head, sem.at[ACT_S], pair_sem.at[k, 1])

    def run(k):
        drain(act_all.at[1 - my_side, k], pair_sem.at[k, 1])
        active = jnp.concatenate([act_all[0, k], act_all[1, k]], axis=0)
        for j in range(n_chip):
            weights = dn_in[per_head * j : per_head * (j + 1)].reshape(wide, units)
            y = dot(active, weights, ((1,), (1,))).astype(BF)
            y_out[j, chunk(k)] = y.reshape(per, ROWS, wide)

        @pl.when(jnp.logical_not(gathers))
        def _():
            send(
                y_out.at[:, chunk(k)],
                y_in.at[:, chunk(k)],
                me,
                mate,
                sem.at[Y_S],
                rs_sem.at[k, 0],
            )

    ring = n_chip == 4
    mid = per // 2
    right, left = lax.rem(chip + 1, n_chip), lax.rem(chip + n_chip - 1, n_chip)

    def rows_of(k, p):
        return pl.ds(k * per + p * mid, mid)

    def to_chip(src, dst, to, sem_in):
        send(src, dst, me, 2 * to + core, sem.at[Z_S], sem_in)

    def add_cores(k):
        drain(y_in.at[:, chunk(k)], rs_sem.at[k, 0])
        for d in (2, 1, 3, 0) if ring else range(n_chip):
            to = lax.rem(chip + d, n_chip)
            z = y_out[to, chunk(k)].astype(F32) + y_in[to, chunk(k)].astype(F32)
            z_out[to, chunk(k)] = z.astype(BF)
            if not ring:
                if d > 0:
                    to_chip(
                        z_out.at[to, chunk(k)], z_in.at[d - 1, chunk(k)], to, rs_sem.at[k, d]
                    )
            elif d == 2:
                for p, side in enumerate((right, left)):
                    view = z_out.at[to, rows_of(k, p)]
                    to_chip(view, z_in.at[2, rows_of(k, p)], side, rs_sem.at[k, 1 + p])
            elif d > 0:
                p = (3 - d) // 2
                view = z_out.at[to, rows_of(k, p)]
                to_chip(view, z_in.at[1 - p, rows_of(k, p)], to, rs_sem.at[k, 3 + p])

    def pass_on(k):
        if ring:
            for p, to in enumerate((right, left)):
                view = z_in.at[2, rows_of(k, p)]
                drain(view, rs_sem.at[k, 1 + p])
                z = z_out[to, rows_of(k, p)].astype(F32) + z_in[2, rows_of(k, p)].astype(F32)
                z_out[to, rows_of(k, p)] = z.astype(BF)
                view = z_out.at[to, rows_of(k, p)]
                to_chip(view, z_in.at[p, rows_of(k, p)], to, rs_sem.at[k, 5 + p])

    def add_chips(k):
        total = z_out[chip, chunk(k)].astype(F32)
        if ring:
            for p in range(2):
                drain(z_in.at[1 - p, rows_of(k, p)], rs_sem.at[k, 3 + p])
                drain(z_in.at[p, rows_of(k, p)], rs_sem.at[k, 5 + p])
            total += z_in[0, chunk(k)].astype(F32) + z_in[1, chunk(k)].astype(F32)
        else:
            for d in range(1, n_chip):
                drain(z_in.at[d - 1, chunk(k)], rs_sem.at[k, d])
                total += z_in[d - 1, chunk(k)].astype(F32)
        ret_out[chunk(k)] = total.astype(BF)

        def give_back(i, carry):
            m = lax.rem(me + 5 * i, per)
            to = CHUNKS * m + lax.rem(k + n_expert - m // 2, CHUNKS)
            row = ret_out.at[k * per + m]

            @pl.when(to != me)
            def _():
                send(row, ret_in.at[my_slot], to, head, sem.at[RET_S], sem.at[RET_R])

            @pl.when(to == me)
            def _():
                pltpu.make_async_copy(row, ret_in.at[my_slot], sem.at[RET_R]).start()

            return carry

        lax.fori_loop(0, per, give_back, 0)

    for stage in range(CHUNKS + 6):
        if 0 <= stage - 2 < CHUNKS:
            activate(stage - 2)
        if stage < CHUNKS:
            part_sums(stage)
            if stage == CHUNKS - 1:
                feed(sent, experts, experts)
        if stage == 3:
            drain(dn_in, sem.at[DN_R])
        if 0 <= stage - 3 < CHUNKS:
            run(stage - 3)
        if stage == CHUNKS + 2:
            send(
                dn_in.at[:, :, lanes_out],
                sync_in.at[my_side],
                partner,
                head,
                sem.at[SYNC_S],
                sem.at[SYNC_R],
            )

        @pl.when(gathers)
        def _():
            for shift, what in ((4, add_cores), (5, pass_on), (6, add_chips)):
                if 0 <= stage - shift < CHUNKS:
                    what(stage - shift)

    sync_in[my_side] = dn_in[:, :, lanes_own]
    drain(sync_in.at[1 - my_side], sem.at[SYNC_R])
    for i in range(n_expert):
        h, r = divmod(i, per_head)
        served = sync_in[h % 2, (h // 2) * per_head + r]
        sync_f[i * block : (i + 1) * block, :] = served.astype(F32)[:block]
    sync_ref[...] = sync_f[...].astype(BF)

    drain(ret_in, sem.at[RET_R])
    returned = ret_in[...].astype(F32).reshape(slots, wide)
    mix = dot(combine, returned, ((0,), (0,)), precision=EXACT)
    mix = dot(mix, stretch.astype(F32), ((1,), (1,)), precision=EXACT)
    out_ref[...] = (hidden + mix).astype(BF).reshape(STEPS, seqs, share)

    others = pl.ds(0, experts - 1)

    @pl.when(keeps_rows)
    def _():
        drain(gu_in.at[others], sem.at[GU_S])
        drain(dn_in.at[others], sem.at[DN_S])

    @pl.when(jnp.logical_not(keeps_rows))
    def _():
        drain(gu_in, sem.at[GU_S])
        drain(dn_in, sem.at[DN_S])

    drain(part_in.at[pl.ds(0, n_head - 1)], sem.at[PART_S])
    drain(square_in.at[pl.ds(0, n_head - 1)], sem.at[SQ_S])
    drain(half_in, sem.at[HALF_S])
    drain(act_all.at[0], sem.at[ACT_S])
    drain(sync_in.at[0], sem.at[SYNC_S])

    @pl.when(gathers)
    def _():
        drain(tok_out.at[others], sem.at[TOK_S])
        drain(tok_all, sem.at[AG_S])
        drain(tok_all.at[pl.ds(0, n_chip - 1)], sem.at[AG_S])
        drain(z_in, sem.at[Z_S])
        drain(ret_out.at[pl.ds(0, n_expert - 1)], sem.at[RET_S])

    @pl.when(jnp.logical_not(gathers))
    def _():
        drain(tok_out, sem.at[TOK_S])
        drain(y_in, sem.at[Y_S])


def local(
    n_expert,
    n_head,
    queries,
    cache_band,
    new_kv,
    cache_lengths,
    sink_logits,
    o_weight,
    residual,
    norm_gain,
    route_logits,
    routes,
    old_experts,
    new_experts,
    train_gate_up,
    train_down,
):
    experts = old_experts.shape[0]
    seqs = queries.shape[1]
    cols = STEPS * seqs
    block = train_gate_up.shape[1]
    padded = -(-block // 16) * 16
    share = residual.shape[2]
    wide = n_expert // n_head * padded
    units = train_gate_up.shape[3]
    half = units // 2
    size = n_expert // CHUNKS * ROWS
    n_chip = n_head // 2
    width = norm_gain.shape[0]
    vmem = pl.BlockSpec(memory_space=pltpu.VMEM)
    out, synced = pl.pallas_call(
        functools.partial(kernel, n_expert, n_head),
        out_shape=(
            jax.ShapeDtypeStruct((STEPS, seqs, share), BF),
            jax.ShapeDtypeStruct((width, half), BF),
        ),
        in_specs=[pl.BlockSpec(memory_space=pltpu.SMEM)] * 2 + [vmem] * 13,
        out_specs=(vmem, vmem),
        scratch_shapes=[
            pltpu.VMEM((2, block * experts, half), F32),
            pltpu.VMEM((experts, padded, 2 * units), BF),
            pltpu.VMEM((experts, padded, units), BF),
            pltpu.VMEM((experts, padded, 2 * units), BF),
            pltpu.VMEM((experts, padded, units), BF),
            pltpu.VMEM((n_head, cols, share), BF),
            pltpu.VMEM((n_head, cols, share), BF),
            pltpu.VMEM((8, cols), F32),
            pltpu.VMEM((n_head, 8, cols), F32),
            pltpu.VMEM((experts, ROWS, wide), BF),
            pltpu.VMEM((n_chip, n_expert, ROWS, wide), BF),
            pltpu.VMEM((CHUNKS, 2, size // 2, 2 * units), F32),
            pltpu.VMEM((CHUNKS, 2, size // 2, 2 * units), BF),
            pltpu.VMEM((CHUNKS, size // 2, 2 * units), BF),
            pltpu.VMEM((2, CHUNKS, size // 2, units), BF),
            pltpu.VMEM((n_chip, n_expert, ROWS, wide), BF),
            pltpu.VMEM((n_chip, n_expert, ROWS, wide), BF),
            pltpu.VMEM((n_chip, n_expert, ROWS, wide), BF),
            pltpu.VMEM((n_chip - 1, n_expert, ROWS, wide), BF),
            pltpu.VMEM((n_expert, ROWS, wide), BF),
            pltpu.VMEM((experts, ROWS, wide), BF),
            pltpu.VMEM((2, experts, padded, half), BF),
            pltpu.VMEM((width, half), F32),
            pltpu.VMEM((TOP, cols), F32),
            pltpu.VMEM((TOP, cols), F32),
            pltpu.SemaphoreType.DMA((18,)),
            pltpu.SemaphoreType.DMA((CHUNKS,)),
            pltpu.SemaphoreType.DMA((CHUNKS, n_chip)),
            pltpu.SemaphoreType.DMA((CHUNKS, 2)),
            pltpu.SemaphoreType.DMA((CHUNKS, 7)),
        ],
        compiler_params=pltpu.CompilerParams(
            collective_id=0, has_side_effects=True, vmem_limit_bytes=56 << 20
        ),
    )(
        old_experts,
        new_experts,
        new_experts.reshape(1, -1),
        cache_lengths.reshape(1, -1),
        sink_logits.reshape(1, -1),
        jnp.transpose(route_logits, (0, 2, 1)),
        jnp.transpose(routes, (0, 2, 1)),
        norm_gain.reshape(1, -1),
        queries,
        cache_band,
        new_kv,
        o_weight.T,
        residual,
        train_gate_up,
        jnp.transpose(train_down, (1, 0, 2)),
    )
    return out, synced[None]


def solution(mesh):
    in_specs = (
        P(None, "expert", "head"),
        P("expert", None, "head"),
        P(None, "expert", "head"),
        P("expert"),
        P("head"),
        P("head", None),
        P(None, "expert", "head"),
        P(),
        P(None, "expert", None),
        P(None, "expert", None),
        P(),
        P(),
        P(None, "expert", None, "head"),
        P(None, "expert", "head"),
    )
    out_specs = (P(None, "expert", "head"), P("expert", None, "head"))
    body = functools.partial(local, mesh.shape["expert"], mesh.shape["head"])
    return jax.shard_map(body, mesh=mesh, in_specs=in_specs, out_specs=out_specs, check_vma=False)
```

```python
import functools
import jax
import jax.numpy as jnp
from jax import lax
from jax.experimental import pallas as pl
from jax.experimental.pallas import tpu as pltpu
from jax.sharding import PartitionSpec as P

HD = 64
TOP = 4
STEPS = 2
GROUP = 4
CAP = 8
ROWS = STEPS * CAP
EPSILON = 1e-05
CHUNKS = 4
STRIDE = 11
FIRST_BATCH = 6
DOWN_EARLY = 16
MESH = pl.DeviceIdType.MESH
BF = jnp.bfloat16
F32 = jnp.float32
EXACT = lax.Precision.HIGHEST


def iota(shape, dim):
    return lax.broadcasted_iota(jnp.int32, shape, dim)


def dot(a, b, dims=((1,), (0,)), precision=None):
    return lax.dot_general(a, b, (dims, ((), ())), preferred_element_type=F32, precision=precision)


def column(row, size):
    eye = iota((size, size), 0) == iota((size, size), 1)
    return jnp.sum(jnp.where(eye, row, 0.0), axis=1, keepdims=True)


def log2(n):
    assert n & (n - 1) == 0
    return n.bit_length() - 1


def kernel(
    n_expert,
    n_head,
    old_slot_ref,
    new_slot_ref,
    new_ref,
    len_ref,
    sink_ref,
    logit_ref,
    route_ref,
    gain_ref,
    query_ref,
    band_hbm,
    new_kv_ref,
    o_hbm,
    residual_ref,
    gate_up_hbm,
    down_hbm,
    out_ref,
    sync_ref,
    down_f,
    gu_out,
    dn_out,
    gu_in,
    dn_in,
    part_out,
    part_in,
    square_out,
    square_in,
    tok_out,
    tok_all,
    half_f,
    half_out,
    half_in,
    act_all,
    y_out,
    y_in,
    z_out,
    z_in,
    ret_out,
    ret_in,
    sync_in,
    sync_f,
    logit_all,
    route_all,
    band_ref,
    o_ref,
    gate_up_ref,
    down_ref,
    load_sem,
    sem,
    tok_sem,
    ag_sem,
    pair_sem,
    rs_sem,
):
    experts = n_expert // 2
    n_chip = n_head // 2
    seqs = query_ref.shape[1]
    cols = STEPS * seqs
    block = gate_up_ref.shape[1]
    padded = gu_in.shape[1]
    share = residual_ref.shape[2]
    per_head = n_expert // n_head
    wide = per_head * padded
    width = n_head * share
    units = gate_up_ref.shape[3]
    half = units // 2
    seq_bits = log2(seqs)
    per = n_expert // CHUNKS

    me = lax.axis_index("expert")
    head = lax.axis_index("head")
    core = lax.rem(head, 2)
    chip = head // 2
    mate = head + 1 - 2 * core
    my_slot = me // 2
    my_side = lax.rem(me, 2)
    partner = me + 1 - 2 * my_side
    row_head = me // per_head
    row_side = lax.rem(row_head, 2)
    row_index = (row_head // 2) * per_head + lax.rem(me, per_head)
    my_chunk = lax.rem(me + me // (2 * CHUNKS), CHUNKS)
    my_spot = my_chunk * per + me // CHUNKS
    gathers = my_side == core
    keeps_rows = my_side == row_side

    loads = [
        pltpu.make_async_copy(a, b, load_sem.at[i])
        for i, (a, b) in enumerate(
            (
                (down_hbm, down_ref),
                (band_hbm, band_ref),
                (o_hbm, o_ref),
                (gate_up_hbm, gate_up_ref),
            )
        )
    ]
    for load in loads:
        load.start()

    barrier = pltpu.get_barrier_semaphore()

    def greet_expert(i, carry):
        pl.semaphore_signal(
            barrier, inc=1, device_id=(lax.rem(me + i, n_expert), head), device_id_type=MESH
        )
        return carry

    def greet_head(i, carry):
        pl.semaphore_signal(
            barrier, inc=1, device_id=(me, lax.rem(head + i, n_head)), device_id_type=MESH
        )
        return carry

    lax.fori_loop(1, n_expert, greet_expert, 0)
    lax.fori_loop(1, n_head, greet_head, 0)

    loads[0].wait()
    for p in range(2):
        down_f[p] = (
            down_ref[:, :, p * half : (p + 1) * half].astype(F32).reshape(block * experts, half)
        )
    pad = padded - block
    last = padded - 16
    gu_out[:, last:, :] = jnp.zeros((experts, 16, 2 * units), BF)
    dn_out[:, last:, :] = jnp.zeros((experts, 16, units), BF)

    GU_S, GU_R, DN_S, DN_R, PART_S, PART_R, SQ_S, SQ_R = range(8)
    TOK_S, AG_S, HALF_S, ACT_S, Y_S, Z_S, RET_S, RET_R, SYNC_S, SYNC_R = range(8, 18)

    def send(src, dst, e, h, s, r):
        pltpu.make_async_remote_copy(
            src_ref=src,
            dst_ref=dst,
            send_sem=s,
            recv_sem=r,
            device_id=(e, h),
            device_id_type=MESH,
        ).start()

    def drain(ref, s):
        pltpu.make_async_copy(ref, ref, s).wait()

    def position(slot):
        expert = new_slot_ref[slot]
        found = jnp.int32(0)
        for k in range(1, experts):
            found = jnp.where(old_slot_ref[k] == expert, k, found)
        return found

    def prepare_gate_up(slot):
        index = position(slot)
        for c in range(2):
            gu_out[slot, :block, c * units : (c + 1) * units] = gate_up_ref[index, :, c, :]

    def prepare_down(slot):
        index = position(slot)
        for p in range(2):
            dn_out[slot, :block, p * half : (p + 1) * half] = down_f[
                p, pl.ds(index, block, stride=experts), :
            ].astype(BF)

    def order(i):
        step = lax.rem(i * STRIDE, experts)
        return lax.rem(my_slot + jnp.where(core == 0, step, experts - step), experts)

    def send_gate_up(i, carry):
        slot = order(i)
        prepare_gate_up(slot)
        to = 2 * slot + row_side
        send(gu_out.at[slot], gu_in.at[row_index], to, head, sem.at[GU_S], sem.at[GU_R])
        return carry

    def send_down(i, carry):
        slot = order(i)
        prepare_down(slot)
        to = 2 * slot + row_side
        send(dn_out.at[slot], dn_in.at[row_index], to, head, sem.at[DN_S], sem.at[DN_R])
        return carry

    lanes = 2 * HD
    rows = STEPS * GROUP * seqs
    r_id = iota((rows, cols), 0)
    c_id = iota((rows, cols), 1)
    same = ((r_id >> 3) == (c_id & (seqs - 1))) & (((r_id >> 2) & 1) == (c_id >> seq_bits))
    rt_id = iota((cols, rows), 1)
    ct_id = iota((cols, rows), 0)
    same_t = ((rt_id >> 3) == (ct_id & (seqs - 1))) & (((rt_id >> 2) & 1) == (ct_id >> seq_bits))
    flat_q = query_ref[...].reshape(cols, GROUP * HD)
    spread_q = jnp.zeros((rows, lanes), F32)
    for g in range(GROUP):
        k_id = iota((GROUP * HD, lanes), 0)
        l_id = iota((GROUP * HD, lanes), 1)
        pick = ((k_id == g * HD + l_id) & (l_id < HD)).astype(BF)
        part = dot(flat_q, pick).astype(BF)
        spread_q += dot((same & ((r_id & 3) == g)).astype(BF), part)
    repeat = ((iota((rows, seqs), 0) >> 3) == iota((rows, seqs), 1)).astype(BF)
    fresh = [dot(repeat, new_kv_ref[s]) for s in range(STEPS)]
    row_s = (iota((rows, 1), 0) >> 2) & 1
    row_g = iota((rows, 1), 0) & 3
    lengths = jnp.sum(
        jnp.where(
            (iota((rows, seqs), 0) >> 3) == iota((rows, seqs), 1), len_ref[...].astype(F32), 0.0
        ),
        axis=1,
        keepdims=True,
    )
    sink = jnp.sum(
        jnp.where(row_g == iota((rows, GROUP), 1), sink_ref[...], 0.0), axis=1, keepdims=True
    )
    scale = HD**-0.5
    loads[1].wait()
    batched = (((2,), (2,)), ((0,), (0,)))
    scores = (
        lax.dot_general(
            spread_q.reshape(seqs, STEPS * GROUP, lanes).astype(BF),
            band_ref[...],
            batched,
            preferred_element_type=F32,
        ).reshape(rows, -1)
        * scale
    )
    window = band_ref.shape[1]
    w_id = iota((rows, window), 1)
    kept = (w_id >= row_s + 1) & (w_id.astype(F32) >= window - lengths)
    scores = jnp.where(kept, scores, -1e30)
    new_scores = [
        jnp.sum(spread_q * fresh[s], axis=1, keepdims=True) * scale for s in range(STEPS)
    ]
    new_scores[1] = jnp.where(row_s == 1, new_scores[1], -1e30)
    top = jnp.maximum(jnp.max(scores, axis=1, keepdims=True), sink)
    top = jnp.maximum(jnp.maximum(top, new_scores[0]), new_scores[1])
    raised = jnp.exp(scores - top)
    new_raised = [jnp.exp(n - top) for n in new_scores]
    total = jnp.sum(raised, axis=1, keepdims=True) + jnp.exp(sink - top)
    total = total + new_raised[0] + new_raised[1]
    probs = (raised / total).reshape(seqs, STEPS * GROUP, window).astype(BF)
    mixed = lax.dot_general(
        probs, band_ref[...], (((2,), (1,)), ((0,), (0,))), preferred_element_type=F32
    ).reshape(rows, lanes)
    for s in range(STEPS):
        mixed += (new_raised[s] / total).astype(BF).astype(F32) * fresh[s]
    mixed = mixed.astype(BF)
    attended = jnp.zeros((cols, GROUP * HD), F32)
    for g in range(GROUP):
        l_id = iota((lanes, GROUP * HD), 0)
        k_id = iota((lanes, GROUP * HD), 1)
        pick = ((k_id - g * HD == l_id - HD) & (l_id >= HD)).astype(BF)
        part = dot(mixed, pick).astype(BF)
        attended += dot((same_t & ((rt_id & 3) == g)).astype(BF), part)
    attended = attended.astype(BF)

    loads[2].wait()
    for j in range(n_head):
        part_out[j] = dot(attended, o_ref[j * share : (j + 1) * share, :], ((1,), (1,))).astype(BF)

    loads[3].wait()
    pl.semaphore_wait(barrier, n_expert + n_head - 2)

    def send_part(i, carry):
        to = lax.rem(head + i, n_head)
        send(part_out.at[to], part_in.at[head], me, to, sem.at[PART_S], sem.at[PART_R])
        return carry

    lax.fori_loop(1, n_head, send_part, 0)
    part_in[head] = part_out[head]

    prepare_gate_up(my_slot)
    prepare_down(my_slot)

    @pl.when(keeps_rows)
    def _():
        pltpu.make_async_copy(gu_out.at[my_slot], gu_in.at[row_index], sem.at[GU_R]).start()
        pltpu.make_async_copy(dn_out.at[my_slot], dn_in.at[row_index], sem.at[DN_R]).start()

    @pl.when(jnp.logical_not(keeps_rows))
    def _():
        send(
            gu_out.at[my_slot], gu_in.at[row_index], partner, head, sem.at[GU_S], sem.at[GU_R]
        )
        send(
            dn_out.at[my_slot], dn_in.at[row_index], partner, head, sem.at[DN_S], sem.at[DN_R]
        )

    lax.fori_loop(1, FIRST_BATCH, send_gate_up, 0)

    new_col = column(new_ref[...].astype(F32), experts)
    for s in range(STEPS):
        logit_all[:, s * seqs : (s + 1) * seqs] = logit_ref[s]
        route_all[:, s * seqs : (s + 1) * seqs] = route_ref[s].astype(F32)
    logits = [logit_all[j : j + 1, :] for j in range(TOP)]
    highest = functools.reduce(jnp.maximum, logits)
    powers = [jnp.exp(l - highest) for l in logits]
    power_sum = functools.reduce(jnp.add, powers)
    member = jnp.zeros((experts, cols), F32)
    weight = jnp.zeros((experts, cols), F32)
    for j in range(TOP):
        hit = (route_all[j : j + 1, :] == new_col).astype(F32)
        member += hit
        weight += hit * (powers[j] / power_sum)
    u0 = iota((cols, cols), 0)
    u1 = iota((cols, cols), 1)
    before = ((u0 < u1) & ((u0 >> seq_bits) == (u1 >> seq_bits))).astype(BF)
    rank = dot(member.astype(BF), before)
    slots = experts * ROWS
    of_slot = ((iota((slots, experts), 0) >> 4) == iota((slots, experts), 1)).astype(BF)
    member_rows = dot(of_slot, member.astype(BF))
    rank_rows = dot(of_slot, rank.astype(BF))
    i_id = iota((slots, cols), 0)
    place = (
        member_rows
        * (rank_rows == (i_id & 7).astype(F32)).astype(F32)
        * (((i_id >> 3) & 1) == (iota((slots, cols), 1) >> seq_bits)).astype(F32)
    )
    combine = dot(of_slot.astype(F32), weight, precision=EXACT) * place

    drain(part_in.at[pl.ds(0, n_head - 1)], sem.at[PART_R])
    hidden = residual_ref[...].reshape(cols, share).astype(F32)
    for j in range(n_head):
        hidden += part_in[j].astype(F32)
    squares = jnp.sum(hidden * hidden, axis=1, keepdims=True)
    square_row = jnp.sum(
        jnp.where(iota((cols, cols), 0) == iota((cols, cols), 1), squares, 0.0),
        axis=0,
        keepdims=True,
    )
    square_out[...] = jnp.broadcast_to(square_row, square_out.shape)

    def send_square(i, carry):
        to = lax.rem(head + i, n_head)
        send(square_out, square_in.at[head], me, to, sem.at[SQ_S], sem.at[SQ_R])
        return carry

    lax.fori_loop(1, n_head, send_square, 0)
    square_in[head] = square_out[...]
    lane = iota((share, wide), 1)
    gap = jnp.zeros((share, wide), jnp.int32)
    for b in range(1, per_head):
        gap += pad * (iota((share, wide), 0) >= b * block).astype(jnp.int32)
    stretch = (iota((share, wide), 0) + gap == lane).astype(BF)
    gain = jnp.zeros((1, share), F32)
    for j in range(n_head):
        gain += jnp.where(head == j, gain_ref[j * share : (j + 1) * share].reshape(1, share), 0.0)
    gained = hidden * gain
    drain(square_in.at[pl.ds(0, n_head - 1)], sem.at[SQ_R])
    all_squares = jnp.zeros((1, cols), F32)
    for j in range(n_head):
        all_squares += square_in[j, 0:1, :]
    norm = column(lax.rsqrt(all_squares * (1.0 / width) + EPSILON), cols)
    token = dot((gained * norm).astype(BF), stretch).astype(BF)
    tok_out[...] = dot(place.astype(BF), token).astype(BF).reshape(experts, ROWS, wide)

    def send_token(i, carry):
        slot = order(i)
        send(
            tok_out.at[slot],
            tok_all.at[chip, my_spot],
            2 * slot + core,
            head,
            sem.at[TOK_S],
            tok_sem.at[my_chunk],
        )
        return carry

    @pl.when(gathers)
    def _():
        pltpu.make_async_copy(
            tok_out.at[my_slot], tok_all.at[chip, my_spot], tok_sem.at[my_chunk]
        ).start()

    @pl.when(jnp.logical_not(gathers))
    def _():
        send(
            tok_out.at[my_slot],
            tok_all.at[chip, my_spot],
            partner,
            head,
            sem.at[TOK_S],
            tok_sem.at[my_chunk],
        )

    lax.fori_loop(1, experts, send_token, 0)

    def feed(sent, count, limit):
        while count and sent[0] < experts:
            n = min(count, experts - sent[0])
            lax.fori_loop(sent[0], sent[0] + n, send_gate_up, 0)
            sent[0] += n
            count -= n
        n = min(count, limit - sent[1])
        if n > 0:
            lax.fori_loop(sent[1], sent[1] + n, send_down, 0)
            sent[1] += n

    def chunk(k):
        return pl.ds(k * per, per)

    @pl.when(gathers)
    def _():
        sent = [FIRST_BATCH, 1]
        feed(sent, 8, DOWN_EARLY)
        for k in range(CHUNKS):
            view = tok_all.at[chip, chunk(k)]
            drain(view, tok_sem.at[k])
            for d in range(1, n_chip):
                to = 2 * lax.rem(chip + d, n_chip) + core
                send(view, view, me, to, sem.at[AG_S], ag_sem.at[k, chip])
            send(view, view, me, mate, sem.at[AG_S], ag_sem.at[k, chip])
            feed(sent, 2, DOWN_EARLY)
        for k in range(CHUNKS):
            for d in range(1, n_chip):
                source = lax.rem(chip + n_chip - d, n_chip)
                view = tok_all.at[source, chunk(k)]
                drain(view, ag_sem.at[k, source])
                send(view, view, me, mate, sem.at[AG_S], ag_sem.at[k, source])
            feed(sent, 5, DOWN_EARLY)
        feed(sent, 2 * experts, DOWN_EARLY)

    @pl.when(jnp.logical_not(gathers))
    def _():
        feed([FIRST_BATCH, 1], 2 * experts, DOWN_EARLY)
        for k in range(CHUNKS):
            for source in range(n_chip):
                drain(tok_all.at[source, chunk(k)], ag_sem.at[k, source])

    drain(gu_in, sem.at[GU_R])
    size = per * ROWS
    part_size = size // 2
    sent = [experts, DOWN_EARLY]
    lanes_out = pl.ds(pl.multiple_of((1 - my_side) * half, half), half)
    lanes_own = pl.ds(pl.multiple_of(my_side * half, half), half)

    def part_sums(k):
        acc = jnp.zeros((size, 2 * units), F32)
        for j in range(0, n_chip, 2):
            rows_in = jnp.concatenate(
                [tok_all[j + i, chunk(k)].reshape(size, wide) for i in range(2)], axis=1
            )
            weights = gu_in[per_head * j : per_head * (j + 2)].reshape(2 * wide, 2 * units)
            acc += dot(rows_in, weights)
        for p in range(2):
            piece = acc[p * part_size : (p + 1) * part_size]
            half_f[k, p] = piece
            half_out[k, p] = piece.astype(BF)
        send(
            half_out.at[k, 1 - my_side],
            half_in.at[k],
            partner,
            head,
            sem.at[HALF_S],
            pair_sem.at[k, 0],
        )
        feed(sent, experts // CHUNKS, experts)

    def activate(k):
        drain(half_in.at[k], pair_sem.at[k, 0])
        acc = half_f[k, my_side] + half_in[k].astype(F32)
        gate = jnp.minimum(acc[:, :units], 7.0)
        up = jnp.clip(acc[:, units:], -7.0, 7.0)
        active = (up + 1.0) * gate * jax.nn.sigmoid(1.702 * gate)
        act_all[my_side, k] = active.astype(BF)
        view = act_all.at[my_side, k]
        send(view, view, partner, head, sem.at[ACT_S], pair_sem.at[k, 1])

    def run(k):
        drain(act_all.at[1 - my_side, k], pair_sem.at[k, 1])
        active = jnp.concatenate([act_all[0, k], act_all[1, k]], axis=0)
        for j in range(n_chip):
            weights = dn_in[per_head * j : per_head * (j + 1)].reshape(wide, units)
            y = dot(active, weights, ((1,), (1,))).astype(BF)
            y_out[j, chunk(k)] = y.reshape(per, ROWS, wide)

        @pl.when(jnp.logical_not(gathers))
        def _():
            send(
                y_out.at[:, chunk(k)],
                y_in.at[:, chunk(k)],
                me,
                mate,
                sem.at[Y_S],
                rs_sem.at[k, 0],
            )

    ring = n_chip == 4
    mid = per // 2
    right, left = lax.rem(chip + 1, n_chip), lax.rem(chip + n_chip - 1, n_chip)

    def rows_of(k, p):
        return pl.ds(k * per + p * mid, mid)

    def to_chip(src, dst, to, sem_in):
        send(src, dst, me, 2 * to + core, sem.at[Z_S], sem_in)

    def add_cores(k):
        drain(y_in.at[:, chunk(k)], rs_sem.at[k, 0])
        for d in (2, 1, 3, 0) if ring else range(n_chip):
            to = lax.rem(chip + d, n_chip)
            z = y_out[to, chunk(k)].astype(F32) + y_in[to, chunk(k)].astype(F32)
            z_out[to, chunk(k)] = z.astype(BF)
            if not ring:
                if d > 0:
                    to_chip(
                        z_out.at[to, chunk(k)], z_in.at[d - 1, chunk(k)], to, rs_sem.at[k, d]
                    )
            elif d == 2:
                for p, side in enumerate((right, left)):
                    view = z_out.at[to, rows_of(k, p)]
                    to_chip(view, z_in.at[2, rows_of(k, p)], side, rs_sem.at[k, 1 + p])
            elif d > 0:
                p = (3 - d) // 2
                view = z_out.at[to, rows_of(k, p)]
                to_chip(view, z_in.at[1 - p, rows_of(k, p)], to, rs_sem.at[k, 3 + p])

    def pass_on(k):
        if ring:
            for p, to in enumerate((right, left)):
                view = z_in.at[2, rows_of(k, p)]
                drain(view, rs_sem.at[k, 1 + p])
                z = z_out[to, rows_of(k, p)].astype(F32) + z_in[2, rows_of(k, p)].astype(F32)
                z_out[to, rows_of(k, p)] = z.astype(BF)
                view = z_out.at[to, rows_of(k, p)]
                to_chip(view, z_in.at[p, rows_of(k, p)], to, rs_sem.at[k, 5 + p])

    def add_chips(k):
        total = z_out[chip, chunk(k)].astype(F32)
        if ring:
            for p in range(2):
                drain(z_in.at[1 - p, rows_of(k, p)], rs_sem.at[k, 3 + p])
                drain(z_in.at[p, rows_of(k, p)], rs_sem.at[k, 5 + p])
            total += z_in[0, chunk(k)].astype(F32) + z_in[1, chunk(k)].astype(F32)
        else:
            for d in range(1, n_chip):
                drain(z_in.at[d - 1, chunk(k)], rs_sem.at[k, d])
                total += z_in[d - 1, chunk(k)].astype(F32)
        ret_out[chunk(k)] = total.astype(BF)

        def give_back(i, carry):
            m = lax.rem(me + 5 * i, per)
            to = CHUNKS * m + lax.rem(k + n_expert - m // 2, CHUNKS)
            row = ret_out.at[k * per + m]

            @pl.when(to != me)
            def _():
                send(row, ret_in.at[my_slot], to, head, sem.at[RET_S], sem.at[RET_R])

            @pl.when(to == me)
            def _():
                pltpu.make_async_copy(row, ret_in.at[my_slot], sem.at[RET_R]).start()

            return carry

        lax.fori_loop(0, per, give_back, 0)

    for stage in range(CHUNKS + 6):
        if 0 <= stage - 2 < CHUNKS:
            activate(stage - 2)
        if stage < CHUNKS:
            part_sums(stage)
            if stage == CHUNKS - 1:
                feed(sent, experts, experts)
        if stage == 3:
            drain(dn_in, sem.at[DN_R])
        if 0 <= stage - 3 < CHUNKS:
            run(stage - 3)
        if stage == CHUNKS + 2:
            send(
                dn_in.at[:, :, lanes_out],
                sync_in.at[my_side],
                partner,
                head,
                sem.at[SYNC_S],
                sem.at[SYNC_R],
            )

        @pl.when(gathers)
        def _():
            for shift, what in ((4, add_cores), (5, pass_on), (6, add_chips)):
                if 0 <= stage - shift < CHUNKS:
                    what(stage - shift)

    sync_in[my_side] = dn_in[:, :, lanes_own]
    drain(sync_in.at[1 - my_side], sem.at[SYNC_R])
    for i in range(n_expert):
        h, r = divmod(i, per_head)
        served = sync_in[h % 2, (h // 2) * per_head + r]
        sync_f[i * block : (i + 1) * block, :] = served.astype(F32)[:block]
    sync_ref[...] = sync_f[...].astype(BF)

    drain(ret_in, sem.at[RET_R])
    returned = ret_in[...].astype(F32).reshape(slots, wide)
    mix = dot(combine, returned, ((0,), (0,)), precision=EXACT)
    mix = dot(mix, stretch.astype(F32), ((1,), (1,)), precision=EXACT)
    out_ref[...] = (hidden + mix).astype(BF).reshape(STEPS, seqs, share)

    others = pl.ds(0, experts - 1)

    @pl.when(keeps_rows)
    def _():
        drain(gu_in.at[others], sem.at[GU_S])
        drain(dn_in.at[others], sem.at[DN_S])

    @pl.when(jnp.logical_not(keeps_rows))
    def _():
        drain(gu_in, sem.at[GU_S])
        drain(dn_in, sem.at[DN_S])

    drain(part_in.at[pl.ds(0, n_head - 1)], sem.at[PART_S])
    drain(square_in.at[pl.ds(0, n_head - 1)], sem.at[SQ_S])
    drain(half_in, sem.at[HALF_S])
    drain(act_all.at[0], sem.at[ACT_S])
    drain(sync_in.at[0], sem.at[SYNC_S])

    @pl.when(gathers)
    def _():
        drain(tok_out.at[others], sem.at[TOK_S])
        drain(tok_all, sem.at[AG_S])
        drain(tok_all.at[pl.ds(0, n_chip - 1)], sem.at[AG_S])
        drain(z_in, sem.at[Z_S])
        drain(ret_out.at[pl.ds(0, n_expert - 1)], sem.at[RET_S])

    @pl.when(jnp.logical_not(gathers))
    def _():
        drain(tok_out, sem.at[TOK_S])
        drain(y_in, sem.at[Y_S])


def local(
    n_expert,
    n_head,
    queries,
    cache_band,
    new_kv,
    cache_lengths,
    sink_logits,
    o_weight,
    residual,
    norm_gain,
    route_logits,
    routes,
    old_experts,
    new_experts,
    train_gate_up,
    train_down,
):
    experts = old_experts.shape[0]
    seqs = queries.shape[1]
    cols = STEPS * seqs
    block = train_gate_up.shape[1]
    padded = -(-block // 16) * 16
    share = residual.shape[2]
    wide = n_expert // n_head * padded
    units = train_gate_up.shape[3]
    half = units // 2
    size = n_expert // CHUNKS * ROWS
    n_chip = n_head // 2
    width = norm_gain.shape[0]
    vmem = pl.BlockSpec(memory_space=pltpu.VMEM)
    hbm = pl.BlockSpec(memory_space=pl.ANY)
    out, synced = pl.pallas_call(
        functools.partial(kernel, n_expert, n_head),
        out_shape=(
            jax.ShapeDtypeStruct((STEPS, seqs, share), BF),
            jax.ShapeDtypeStruct((width, half), BF),
        ),
        in_specs=[pl.BlockSpec(memory_space=pltpu.SMEM)] * 2
        + [vmem] * 7
        + [hbm, vmem, hbm, vmem, hbm, hbm],
        out_specs=(vmem, vmem),
        scratch_shapes=[
            pltpu.VMEM((2, block * experts, half), F32),
            pltpu.VMEM((experts, padded, 2 * units), BF),
            pltpu.VMEM((experts, padded, units), BF),
            pltpu.VMEM((experts, padded, 2 * units), BF),
            pltpu.VMEM((experts, padded, units), BF),
            pltpu.VMEM((n_head, cols, share), BF),
            pltpu.VMEM((n_head, cols, share), BF),
            pltpu.VMEM((8, cols), F32),
            pltpu.VMEM((n_head, 8, cols), F32),
            pltpu.VMEM((experts, ROWS, wide), BF),
            pltpu.VMEM((n_chip, n_expert, ROWS, wide), BF),
            pltpu.VMEM((CHUNKS, 2, size // 2, 2 * units), F32),
            pltpu.VMEM((CHUNKS, 2, size // 2, 2 * units), BF),
            pltpu.VMEM((CHUNKS, size // 2, 2 * units), BF),
            pltpu.VMEM((2, CHUNKS, size // 2, units), BF),
            pltpu.VMEM((n_chip, n_expert, ROWS, wide), BF),
            pltpu.VMEM((n_chip, n_expert, ROWS, wide), BF),
            pltpu.VMEM((n_chip, n_expert, ROWS, wide), BF),
            pltpu.VMEM((n_chip - 1, n_expert, ROWS, wide), BF),
            pltpu.VMEM((n_expert, ROWS, wide), BF),
            pltpu.VMEM((experts, ROWS, wide), BF),
            pltpu.VMEM((2, experts, padded, half), BF),
            pltpu.VMEM((width, half), F32),
            pltpu.VMEM((TOP, cols), F32),
            pltpu.VMEM((TOP, cols), F32),
            pltpu.VMEM(cache_band.shape, BF),
            pltpu.VMEM(o_weight.shape[::-1], BF),
            pltpu.VMEM(train_gate_up.shape, BF),
            pltpu.VMEM((block, experts, units), BF),
            pltpu.SemaphoreType.DMA((4,)),
            pltpu.SemaphoreType.DMA((18,)),
            pltpu.SemaphoreType.DMA((CHUNKS,)),
            pltpu.SemaphoreType.DMA((CHUNKS, n_chip)),
            pltpu.SemaphoreType.DMA((CHUNKS, 2)),
            pltpu.SemaphoreType.DMA((CHUNKS, 7)),
        ],
        compiler_params=pltpu.CompilerParams(
            collective_id=0, has_side_effects=True, vmem_limit_bytes=56 << 20
        ),
    )(
        old_experts,
        new_experts,
        new_experts.reshape(1, -1),
        cache_lengths.reshape(1, -1),
        sink_logits.reshape(1, -1),
        jnp.transpose(route_logits, (0, 2, 1)),
        jnp.transpose(routes, (0, 2, 1)),
        norm_gain,
        queries,
        cache_band,
        new_kv,
        o_weight.T,
        residual,
        train_gate_up,
        jnp.transpose(train_down, (1, 0, 2)),
    )
    return out, synced[None]


def solution(mesh):
    in_specs = (
        P(None, "expert", "head"),
        P("expert", None, "head"),
        P(None, "expert", "head"),
        P("expert"),
        P("head"),
        P("head", None),
        P(None, "expert", "head"),
        P(),
        P(None, "expert", None),
        P(None, "expert", None),
        P(),
        P(),
        P(None, "expert", None, "head"),
        P(None, "expert", "head"),
    )
    out_specs = (P(None, "expert", "head"), P("expert", None, "head"))
    body = functools.partial(local, mesh.shape["expert"], mesh.shape["head"])
    return jax.shard_map(body, mesh=mesh, in_specs=in_specs, out_specs=out_specs, check_vma=False)
```

```python
import functools
import jax
import jax.numpy as jnp
from jax import lax
from jax.experimental import pallas as pl
from jax.experimental.pallas import tpu as pltpu
from jax.sharding import PartitionSpec as P

HD = 64
TOP = 4
STEPS = 2
GROUP = 4
CAP = 8
ROWS = STEPS * CAP
EPSILON = 1e-05
CHUNKS = 4
STRIDE = 9
FIRST_BATCH = 6
DOWN_EARLY = 16
MESH = pl.DeviceIdType.MESH
BF = jnp.bfloat16
F32 = jnp.float32
EXACT = lax.Precision.HIGHEST


def iota(shape, dim):
    return lax.broadcasted_iota(jnp.int32, shape, dim)


def dot(a, b, dims=((1,), (0,)), precision=None):
    return lax.dot_general(a, b, (dims, ((), ())), preferred_element_type=F32, precision=precision)


def column(row, size):
    eye = iota((size, size), 0) == iota((size, size), 1)
    return jnp.sum(jnp.where(eye, row, 0.0), axis=1, keepdims=True)


def log2(n):
    assert n & (n - 1) == 0
    return n.bit_length() - 1


def kernel(
    n_expert,
    n_head,
    old_slot_ref,
    new_slot_ref,
    new_ref,
    len_ref,
    sink_ref,
    logit_ref,
    route_ref,
    gain_ref,
    query_ref,
    band_hbm,
    new_kv_ref,
    o_hbm,
    residual_ref,
    gate_up_hbm,
    down_hbm,
    out_ref,
    sync_ref,
    down_f,
    gu_out,
    dn_out,
    gu_in,
    dn_in,
    part_out,
    part_in,
    square_out,
    square_in,
    tok_out,
    tok_all,
    half_f,
    half_out,
    half_in,
    act_all,
    y_out,
    y_in,
    z_out,
    z_in,
    ret_out,
    ret_in,
    sync_in,
    sync_f,
    logit_all,
    route_all,
    band_ref,
    o_ref,
    gate_up_ref,
    down_ref,
    load_sem,
    sem,
    tok_sem,
    ag_sem,
    pair_sem,
    rs_sem,
):
    experts = n_expert // 2
    n_chip = n_head // 2
    seqs = query_ref.shape[1]
    cols = STEPS * seqs
    block = gate_up_ref.shape[1]
    padded = gu_in.shape[1]
    share = residual_ref.shape[2]
    per_head = n_expert // n_head
    wide = per_head * padded
    width = n_head * share
    units = gate_up_ref.shape[3]
    half = units // 2
    seq_bits = log2(seqs)
    per = n_expert // CHUNKS

    me = lax.axis_index("expert")
    head = lax.axis_index("head")
    core = lax.rem(head, 2)
    chip = head // 2
    mate = head + 1 - 2 * core
    my_slot = me // 2
    my_side = lax.rem(me, 2)
    partner = me + 1 - 2 * my_side
    row_head = me // per_head
    row_side = lax.rem(row_head, 2)
    row_index = (row_head // 2) * per_head + lax.rem(me, per_head)
    my_chunk = lax.rem(me + me // (2 * CHUNKS), CHUNKS)
    my_spot = my_chunk * per + me // CHUNKS
    gathers = my_side == core
    keeps_rows = my_side == row_side

    loads = [
        pltpu.make_async_copy(a, b, load_sem.at[i])
        for i, (a, b) in enumerate(
            (
                (down_hbm, down_ref),
                (band_hbm, band_ref),
                (o_hbm, o_ref),
                (gate_up_hbm, gate_up_ref),
            )
        )
    ]
    for load in loads:
        load.start()

    barrier = pltpu.get_barrier_semaphore()

    def greet_expert(i, carry):
        pl.semaphore_signal(
            barrier, inc=1, device_id=(lax.rem(me + i, n_expert), head), device_id_type=MESH
        )
        return carry

    def greet_head(i, carry):
        pl.semaphore_signal(
            barrier, inc=1, device_id=(me, lax.rem(head + i, n_head)), device_id_type=MESH
        )
        return carry

    lax.fori_loop(1, n_expert, greet_expert, 0)
    lax.fori_loop(1, n_head, greet_head, 0)

    loads[0].wait()
    for p in range(2):
        down_f[p] = (
            down_ref[:, :, p * half : (p + 1) * half].astype(F32).reshape(block * experts, half)
        )
    pad = padded - block
    last = padded - 16
    gu_out[:, last:, :] = jnp.zeros((experts, 16, 2 * units), BF)
    dn_out[:, last:, :] = jnp.zeros((experts, 16, units), BF)

    GU_S, GU_R, DN_S, DN_R, PART_S, PART_R, SQ_S, SQ_R = range(8)
    TOK_S, AG_S, HALF_S, ACT_S, Y_S, Z_S, RET_S, RET_R, SYNC_S, SYNC_R = range(8, 18)

    def send(src, dst, e, h, s, r):
        pltpu.make_async_remote_copy(
            src_ref=src,
            dst_ref=dst,
            send_sem=s,
            recv_sem=r,
            device_id=(e, h),
            device_id_type=MESH,
        ).start()

    def drain(ref, s):
        pltpu.make_async_copy(ref, ref, s).wait()

    def position(slot):
        expert = new_slot_ref[slot]
        found = jnp.int32(0)
        for k in range(1, experts):
            found = jnp.where(old_slot_ref[k] == expert, k, found)
        return found

    def prepare_gate_up(slot):
        index = position(slot)
        for c in range(2):
            gu_out[slot, :block, c * units : (c + 1) * units] = gate_up_ref[index, :, c, :]

    def prepare_down(slot):
        index = position(slot)
        for p in range(2):
            dn_out[slot, :block, p * half : (p + 1) * half] = down_f[
                p, pl.ds(index, block, stride=experts), :
            ].astype(BF)

    def order(i):
        step = lax.rem(i * STRIDE, experts)
        return lax.rem(my_slot + jnp.where(core == 0, step, experts - step), experts)

    def send_gate_up(i, carry):
        slot = order(i)
        prepare_gate_up(slot)
        to = 2 * slot + row_side
        send(gu_out.at[slot], gu_in.at[row_index], to, head, sem.at[GU_S], sem.at[GU_R])
        return carry

    def send_down(i, carry):
        slot = order(i)
        prepare_down(slot)
        to = 2 * slot + row_side
        send(dn_out.at[slot], dn_in.at[row_index], to, head, sem.at[DN_S], sem.at[DN_R])
        return carry

    lanes = 2 * HD
    rows = STEPS * GROUP * seqs
    r_id = iota((rows, cols), 0)
    c_id = iota((rows, cols), 1)
    same = ((r_id >> 3) == (c_id & (seqs - 1))) & (((r_id >> 2) & 1) == (c_id >> seq_bits))
    rt_id = iota((cols, rows), 1)
    ct_id = iota((cols, rows), 0)
    same_t = ((rt_id >> 3) == (ct_id & (seqs - 1))) & (((rt_id >> 2) & 1) == (ct_id >> seq_bits))
    flat_q = query_ref[...].reshape(cols, GROUP * HD)
    spread_q = jnp.zeros((rows, lanes), F32)
    for g in range(GROUP):
        k_id = iota((GROUP * HD, lanes), 0)
        l_id = iota((GROUP * HD, lanes), 1)
        pick = ((k_id == g * HD + l_id) & (l_id < HD)).astype(BF)
        part = dot(flat_q, pick).astype(BF)
        spread_q += dot((same & ((r_id & 3) == g)).astype(BF), part)
    repeat = ((iota((rows, seqs), 0) >> 3) == iota((rows, seqs), 1)).astype(BF)
    fresh = [dot(repeat, new_kv_ref[s]) for s in range(STEPS)]
    row_s = (iota((rows, 1), 0) >> 2) & 1
    row_g = iota((rows, 1), 0) & 3
    lengths = jnp.sum(
        jnp.where(
            (iota((rows, seqs), 0) >> 3) == iota((rows, seqs), 1), len_ref[...].astype(F32), 0.0
        ),
        axis=1,
        keepdims=True,
    )
    sink = jnp.sum(
        jnp.where(row_g == iota((rows, GROUP), 1), sink_ref[...], 0.0), axis=1, keepdims=True
    )
    scale = HD**-0.5
    loads[1].wait()
    batched = (((2,), (2,)), ((0,), (0,)))
    scores = (
        lax.dot_general(
            spread_q.reshape(seqs, STEPS * GROUP, lanes).astype(BF),
            band_ref[...],
            batched,
            preferred_element_type=F32,
        ).reshape(rows, -1)
        * scale
    )
    window = band_ref.shape[1]
    w_id = iota((rows, window), 1)
    kept = (w_id >= row_s + 1) & (w_id.astype(F32) >= window - lengths)
    scores = jnp.where(kept, scores, -1e30)
    new_scores = [
        jnp.sum(spread_q * fresh[s], axis=1, keepdims=True) * scale for s in range(STEPS)
    ]
    new_scores[1] = jnp.where(row_s == 1, new_scores[1], -1e30)
    top = jnp.maximum(jnp.max(scores, axis=1, keepdims=True), sink)
    top = jnp.maximum(jnp.maximum(top, new_scores[0]), new_scores[1])
    raised = jnp.exp(scores - top)
    new_raised = [jnp.exp(n - top) for n in new_scores]
    total = jnp.sum(raised, axis=1, keepdims=True) + jnp.exp(sink - top)
    total = total + new_raised[0] + new_raised[1]
    probs = (raised / total).reshape(seqs, STEPS * GROUP, window).astype(BF)
    mixed = lax.dot_general(
        probs, band_ref[...], (((2,), (1,)), ((0,), (0,))), preferred_element_type=F32
    ).reshape(rows, lanes)
    for s in range(STEPS):
        mixed += (new_raised[s] / total).astype(BF).astype(F32) * fresh[s]
    mixed = mixed.astype(BF)
    attended = jnp.zeros((cols, GROUP * HD), F32)
    for g in range(GROUP):
        l_id = iota((lanes, GROUP * HD), 0)
        k_id = iota((lanes, GROUP * HD), 1)
        pick = ((k_id - g * HD == l_id - HD) & (l_id >= HD)).astype(BF)
        part = dot(mixed, pick).astype(BF)
        attended += dot((same_t & ((rt_id & 3) == g)).astype(BF), part)
    attended = attended.astype(BF)

    loads[2].wait()
    for j in range(n_head):
        part_out[j] = dot(attended, o_ref[j * share : (j + 1) * share, :], ((1,), (1,))).astype(BF)

    loads[3].wait()
    pl.semaphore_wait(barrier, n_expert + n_head - 2)

    def send_part(i, carry):
        to = lax.rem(head + i, n_head)
        send(part_out.at[to], part_in.at[head], me, to, sem.at[PART_S], sem.at[PART_R])
        return carry

    lax.fori_loop(1, n_head, send_part, 0)
    part_in[head] = part_out[head]

    prepare_gate_up(my_slot)
    prepare_down(my_slot)

    @pl.when(keeps_rows)
    def _():
        pltpu.make_async_copy(gu_out.at[my_slot], gu_in.at[row_index], sem.at[GU_R]).start()
        pltpu.make_async_copy(dn_out.at[my_slot], dn_in.at[row_index], sem.at[DN_R]).start()

    @pl.when(jnp.logical_not(keeps_rows))
    def _():
        send(
            gu_out.at[my_slot], gu_in.at[row_index], partner, head, sem.at[GU_S], sem.at[GU_R]
        )
        send(
            dn_out.at[my_slot], dn_in.at[row_index], partner, head, sem.at[DN_S], sem.at[DN_R]
        )

    lax.fori_loop(1, FIRST_BATCH, send_gate_up, 0)

    new_col = column(new_ref[...].astype(F32), experts)
    for s in range(STEPS):
        logit_all[:, s * seqs : (s + 1) * seqs] = logit_ref[s]
        route_all[:, s * seqs : (s + 1) * seqs] = route_ref[s].astype(F32)
    logits = [logit_all[j : j + 1, :] for j in range(TOP)]
    highest = functools.reduce(jnp.maximum, logits)
    powers = [jnp.exp(l - highest) for l in logits]
    power_sum = functools.reduce(jnp.add, powers)
    member = jnp.zeros((experts, cols), F32)
    weight = jnp.zeros((experts, cols), F32)
    for j in range(TOP):
        hit = (route_all[j : j + 1, :] == new_col).astype(F32)
        member += hit
        weight += hit * (powers[j] / power_sum)
    u0 = iota((cols, cols), 0)
    u1 = iota((cols, cols), 1)
    before = ((u0 < u1) & ((u0 >> seq_bits) == (u1 >> seq_bits))).astype(BF)
    rank = dot(member.astype(BF), before)
    slots = experts * ROWS
    of_slot = ((iota((slots, experts), 0) >> 4) == iota((slots, experts), 1)).astype(BF)
    member_rows = dot(of_slot, member.astype(BF))
    rank_rows = dot(of_slot, rank.astype(BF))
    i_id = iota((slots, cols), 0)
    place = (
        member_rows
        * (rank_rows == (i_id & 7).astype(F32)).astype(F32)
        * (((i_id >> 3) & 1) == (iota((slots, cols), 1) >> seq_bits)).astype(F32)
    )
    combine = dot(of_slot.astype(F32), weight, precision=EXACT) * place

    drain(part_in.at[pl.ds(0, n_head - 1)], sem.at[PART_R])
    hidden = residual_ref[...].reshape(cols, share).astype(F32)
    for j in range(n_head):
        hidden += part_in[j].astype(F32)
    squares = jnp.sum(hidden * hidden, axis=1, keepdims=True)
    square_row = jnp.sum(
        jnp.where(iota((cols, cols), 0) == iota((cols, cols), 1), squares, 0.0),
        axis=0,
        keepdims=True,
    )
    square_out[...] = jnp.broadcast_to(square_row, square_out.shape)

    def send_square(i, carry):
        to = lax.rem(head + i, n_head)
        send(square_out, square_in.at[head], me, to, sem.at[SQ_S], sem.at[SQ_R])
        return carry

    lax.fori_loop(1, n_head, send_square, 0)
    square_in[head] = square_out[...]
    lane = iota((share, wide), 1)
    gap = jnp.zeros((share, wide), jnp.int32)
    for b in range(1, per_head):
        gap += pad * (iota((share, wide), 0) >= b * block).astype(jnp.int32)
    stretch = (iota((share, wide), 0) + gap == lane).astype(BF)
    gain = jnp.zeros((1, share), F32)
    for j in range(n_head):
        gain += jnp.where(head == j, gain_ref[j * share : (j + 1) * share].reshape(1, share), 0.0)
    gained = hidden * gain
    drain(square_in.at[pl.ds(0, n_head - 1)], sem.at[SQ_R])
    all_squares = jnp.zeros((1, cols), F32)
    for j in range(n_head):
        all_squares += square_in[j, 0:1, :]
    norm = column(lax.rsqrt(all_squares * (1.0 / width) + EPSILON), cols)
    token = dot((gained * norm).astype(BF), stretch).astype(BF)
    tok_out[...] = dot(place.astype(BF), token).astype(BF).reshape(experts, ROWS, wide)

    def send_token(i, carry):
        slot = order(i)
        send(
            tok_out.at[slot],
            tok_all.at[chip, my_spot],
            2 * slot + core,
            head,
            sem.at[TOK_S],
            tok_sem.at[my_chunk],
        )
        return carry

    @pl.when(gathers)
    def _():
        pltpu.make_async_copy(
            tok_out.at[my_slot], tok_all.at[chip, my_spot], tok_sem.at[my_chunk]
        ).start()

    @pl.when(jnp.logical_not(gathers))
    def _():
        send(
            tok_out.at[my_slot],
            tok_all.at[chip, my_spot],
            partner,
            head,
            sem.at[TOK_S],
            tok_sem.at[my_chunk],
        )

    lax.fori_loop(1, experts, send_token, 0)

    def feed(sent, count, limit):
        while count and sent[0] < experts:
            n = min(count, experts - sent[0])
            lax.fori_loop(sent[0], sent[0] + n, send_gate_up, 0)
            sent[0] += n
            count -= n
        n = min(count, limit - sent[1])
        if n > 0:
            lax.fori_loop(sent[1], sent[1] + n, send_down, 0)
            sent[1] += n

    def chunk(k):
        return pl.ds(k * per, per)

    @pl.when(gathers)
    def _():
        sent = [FIRST_BATCH, 1]
        feed(sent, 8, DOWN_EARLY)
        for k in range(CHUNKS):
            view = tok_all.at[chip, chunk(k)]
            drain(view, tok_sem.at[k])
            for d in range(1, n_chip):
                to = 2 * lax.rem(chip + d, n_chip) + core
                send(view, view, me, to, sem.at[AG_S], ag_sem.at[k, chip])
            send(view, view, me, mate, sem.at[AG_S], ag_sem.at[k, chip])
            feed(sent, 2, DOWN_EARLY)
        for k in range(CHUNKS):
            for d in range(1, n_chip):
                source = lax.rem(chip + n_chip - d, n_chip)
                view = tok_all.at[source, chunk(k)]
                drain(view, ag_sem.at[k, source])
                send(view, view, me, mate, sem.at[AG_S], ag_sem.at[k, source])
            feed(sent, 5, DOWN_EARLY)
        feed(sent, 2 * experts, DOWN_EARLY)

    @pl.when(jnp.logical_not(gathers))
    def _():
        feed([FIRST_BATCH, 1], 2 * experts, DOWN_EARLY)
        for k in range(CHUNKS):
            for source in range(n_chip):
                drain(tok_all.at[source, chunk(k)], ag_sem.at[k, source])

    drain(gu_in, sem.at[GU_R])
    size = per * ROWS
    part_size = size // 2
    sent = [experts, DOWN_EARLY]
    lanes_out = pl.ds(pl.multiple_of((1 - my_side) * half, half), half)
    lanes_own = pl.ds(pl.multiple_of(my_side * half, half), half)

    def part_sums(k):
        acc = jnp.zeros((size, 2 * units), F32)
        for j in range(0, n_chip, 2):
            rows_in = jnp.concatenate(
                [tok_all[j + i, chunk(k)].reshape(size, wide) for i in range(2)], axis=1
            )
            weights = gu_in[per_head * j : per_head * (j + 2)].reshape(2 * wide, 2 * units)
            acc += dot(rows_in, weights)
        for p in range(2):
            piece = acc[p * part_size : (p + 1) * part_size]
            half_f[k, p] = piece
            half_out[k, p] = piece.astype(BF)
        send(
            half_out.at[k, 1 - my_side],
            half_in.at[k],
            partner,
            head,
            sem.at[HALF_S],
            pair_sem.at[k, 0],
        )
        feed(sent, experts // CHUNKS, experts)

    def activate(k):
        drain(half_in.at[k], pair_sem.at[k, 0])
        acc = half_f[k, my_side] + half_in[k].astype(F32)
        gate = jnp.minimum(acc[:, :units], 7.0)
        up = jnp.clip(acc[:, units:], -7.0, 7.0)
        active = (up + 1.0) * gate * jax.nn.sigmoid(1.702 * gate)
        act_all[my_side, k] = active.astype(BF)
        view = act_all.at[my_side, k]
        send(view, view, partner, head, sem.at[ACT_S], pair_sem.at[k, 1])

    def run(k):
        drain(act_all.at[1 - my_side, k], pair_sem.at[k, 1])
        active = jnp.concatenate([act_all[0, k], act_all[1, k]], axis=0)
        for j in range(n_chip):
            weights = dn_in[per_head * j : per_head * (j + 1)].reshape(wide, units)
            y = dot(active, weights, ((1,), (1,))).astype(BF)
            y_out[j, chunk(k)] = y.reshape(per, ROWS, wide)

        @pl.when(jnp.logical_not(gathers))
        def _():
            send(
                y_out.at[:, chunk(k)],
                y_in.at[:, chunk(k)],
                me,
                mate,
                sem.at[Y_S],
                rs_sem.at[k, 0],
            )

    ring = n_chip == 4
    mid = per // 2
    right, left = lax.rem(chip + 1, n_chip), lax.rem(chip + n_chip - 1, n_chip)

    def rows_of(k, p):
        return pl.ds(k * per + p * mid, mid)

    def to_chip(src, dst, to, sem_in):
        send(src, dst, me, 2 * to + core, sem.at[Z_S], sem_in)

    def add_cores(k):
        drain(y_in.at[:, chunk(k)], rs_sem.at[k, 0])
        for d in (2, 1, 3, 0) if ring else range(n_chip):
            to = lax.rem(chip + d, n_chip)
            z = y_out[to, chunk(k)].astype(F32) + y_in[to, chunk(k)].astype(F32)
            z_out[to, chunk(k)] = z.astype(BF)
            if not ring:
                if d > 0:
                    to_chip(
                        z_out.at[to, chunk(k)], z_in.at[d - 1, chunk(k)], to, rs_sem.at[k, d]
                    )
            elif d == 2:
                for p, side in enumerate((right, left)):
                    view = z_out.at[to, rows_of(k, p)]
                    to_chip(view, z_in.at[2, rows_of(k, p)], side, rs_sem.at[k, 1 + p])
            elif d > 0:
                p = (3 - d) // 2
                view = z_out.at[to, rows_of(k, p)]
                to_chip(view, z_in.at[1 - p, rows_of(k, p)], to, rs_sem.at[k, 3 + p])

    def pass_on(k):
        if ring:
            for p, to in enumerate((right, left)):
                view = z_in.at[2, rows_of(k, p)]
                drain(view, rs_sem.at[k, 1 + p])
                z = z_out[to, rows_of(k, p)].astype(F32) + z_in[2, rows_of(k, p)].astype(F32)
                z_out[to, rows_of(k, p)] = z.astype(BF)
                view = z_out.at[to, rows_of(k, p)]
                to_chip(view, z_in.at[p, rows_of(k, p)], to, rs_sem.at[k, 5 + p])

    def add_chips(k):
        total = z_out[chip, chunk(k)].astype(F32)
        if ring:
            for p in range(2):
                drain(z_in.at[1 - p, rows_of(k, p)], rs_sem.at[k, 3 + p])
                drain(z_in.at[p, rows_of(k, p)], rs_sem.at[k, 5 + p])
            total += z_in[0, chunk(k)].astype(F32) + z_in[1, chunk(k)].astype(F32)
        else:
            for d in range(1, n_chip):
                drain(z_in.at[d - 1, chunk(k)], rs_sem.at[k, d])
                total += z_in[d - 1, chunk(k)].astype(F32)
        ret_out[chunk(k)] = total.astype(BF)

        def give_back(i, carry):
            m = lax.rem(me + 5 * i, per)
            to = CHUNKS * m + lax.rem(k + n_expert - m // 2, CHUNKS)
            row = ret_out.at[k * per + m]

            @pl.when(to != me)
            def _():
                send(row, ret_in.at[my_slot], to, head, sem.at[RET_S], sem.at[RET_R])

            @pl.when(to == me)
            def _():
                pltpu.make_async_copy(row, ret_in.at[my_slot], sem.at[RET_R]).start()

            return carry

        lax.fori_loop(0, per, give_back, 0)

    for stage in range(CHUNKS + 6):
        if 0 <= stage - 2 < CHUNKS:
            activate(stage - 2)
        if stage < CHUNKS:
            part_sums(stage)
            if stage == CHUNKS - 1:
                feed(sent, experts, experts)
        if stage == 3:
            drain(dn_in, sem.at[DN_R])
        if 0 <= stage - 3 < CHUNKS:
            run(stage - 3)
        if stage == CHUNKS + 2:
            send(
                dn_in.at[:, :, lanes_out],
                sync_in.at[my_side],
                partner,
                head,
                sem.at[SYNC_S],
                sem.at[SYNC_R],
            )

        @pl.when(gathers)
        def _():
            for shift, what in ((4, add_cores), (5, pass_on), (6, add_chips)):
                if 0 <= stage - shift < CHUNKS:
                    what(stage - shift)

    sync_in[my_side] = dn_in[:, :, lanes_own]
    drain(sync_in.at[1 - my_side], sem.at[SYNC_R])
    for i in range(n_expert):
        h, r = divmod(i, per_head)
        served = sync_in[h % 2, (h // 2) * per_head + r]
        sync_f[i * block : (i + 1) * block, :] = served.astype(F32)[:block]
    sync_ref[...] = sync_f[...].astype(BF)

    drain(ret_in, sem.at[RET_R])
    returned = ret_in[...].astype(F32).reshape(slots, wide)
    mix = dot(combine, returned, ((0,), (0,)), precision=EXACT)
    mix = dot(mix, stretch.astype(F32), ((1,), (1,)), precision=EXACT)
    out_ref[...] = (hidden + mix).astype(BF).reshape(STEPS, seqs, share)

    others = pl.ds(0, experts - 1)

    @pl.when(keeps_rows)
    def _():
        drain(gu_in.at[others], sem.at[GU_S])
        drain(dn_in.at[others], sem.at[DN_S])

    @pl.when(jnp.logical_not(keeps_rows))
    def _():
        drain(gu_in, sem.at[GU_S])
        drain(dn_in, sem.at[DN_S])

    drain(part_in.at[pl.ds(0, n_head - 1)], sem.at[PART_S])
    drain(square_in.at[pl.ds(0, n_head - 1)], sem.at[SQ_S])
    drain(half_in, sem.at[HALF_S])
    drain(act_all.at[0], sem.at[ACT_S])
    drain(sync_in.at[0], sem.at[SYNC_S])

    @pl.when(gathers)
    def _():
        drain(tok_out.at[others], sem.at[TOK_S])
        drain(tok_all, sem.at[AG_S])
        drain(tok_all.at[pl.ds(0, n_chip - 1)], sem.at[AG_S])
        drain(z_in, sem.at[Z_S])
        drain(ret_out.at[pl.ds(0, n_expert - 1)], sem.at[RET_S])

    @pl.when(jnp.logical_not(gathers))
    def _():
        drain(tok_out, sem.at[TOK_S])
        drain(y_in, sem.at[Y_S])


def local(
    n_expert,
    n_head,
    queries,
    cache_band,
    new_kv,
    cache_lengths,
    sink_logits,
    o_weight,
    residual,
    norm_gain,
    route_logits,
    routes,
    old_experts,
    new_experts,
    train_gate_up,
    train_down,
):
    experts = old_experts.shape[0]
    seqs = queries.shape[1]
    cols = STEPS * seqs
    block = train_gate_up.shape[1]
    padded = -(-block // 16) * 16
    share = residual.shape[2]
    wide = n_expert // n_head * padded
    units = train_gate_up.shape[3]
    half = units // 2
    size = n_expert // CHUNKS * ROWS
    n_chip = n_head // 2
    width = norm_gain.shape[0]
    vmem = pl.BlockSpec(memory_space=pltpu.VMEM)
    hbm = pl.BlockSpec(memory_space=pl.ANY)
    out, synced = pl.pallas_call(
        functools.partial(kernel, n_expert, n_head),
        out_shape=(
            jax.ShapeDtypeStruct((STEPS, seqs, share), BF),
            jax.ShapeDtypeStruct((width, half), BF),
        ),
        in_specs=[pl.BlockSpec(memory_space=pltpu.SMEM)] * 2
        + [vmem] * 7
        + [hbm, vmem, hbm, vmem, hbm, hbm],
        out_specs=(vmem, vmem),
        scratch_shapes=[
            pltpu.VMEM((2, block * experts, half), F32),
            pltpu.VMEM((experts, padded, 2 * units), BF),
            pltpu.VMEM((experts, padded, units), BF),
            pltpu.VMEM((experts, padded, 2 * units), BF),
            pltpu.VMEM((experts, padded, units), BF),
            pltpu.VMEM((n_head, cols, share), BF),
            pltpu.VMEM((n_head, cols, share), BF),
            pltpu.VMEM((8, cols), F32),
            pltpu.VMEM((n_head, 8, cols), F32),
            pltpu.VMEM((experts, ROWS, wide), BF),
            pltpu.VMEM((n_chip, n_expert, ROWS, wide), BF),
            pltpu.VMEM((CHUNKS, 2, size // 2, 2 * units), F32),
            pltpu.VMEM((CHUNKS, 2, size // 2, 2 * units), BF),
            pltpu.VMEM((CHUNKS, size // 2, 2 * units), BF),
            pltpu.VMEM((2, CHUNKS, size // 2, units), BF),
            pltpu.VMEM((n_chip, n_expert, ROWS, wide), BF),
            pltpu.VMEM((n_chip, n_expert, ROWS, wide), BF),
            pltpu.VMEM((n_chip, n_expert, ROWS, wide), BF),
            pltpu.VMEM((n_chip - 1, n_expert, ROWS, wide), BF),
            pltpu.VMEM((n_expert, ROWS, wide), BF),
            pltpu.VMEM((experts, ROWS, wide), BF),
            pltpu.VMEM((2, experts, padded, half), BF),
            pltpu.VMEM((width, half), F32),
            pltpu.VMEM((TOP, cols), F32),
            pltpu.VMEM((TOP, cols), F32),
            pltpu.VMEM(cache_band.shape, BF),
            pltpu.VMEM(o_weight.shape[::-1], BF),
            pltpu.VMEM(train_gate_up.shape, BF),
            pltpu.VMEM((block, experts, units), BF),
            pltpu.SemaphoreType.DMA((4,)),
            pltpu.SemaphoreType.DMA((18,)),
            pltpu.SemaphoreType.DMA((CHUNKS,)),
            pltpu.SemaphoreType.DMA((CHUNKS, n_chip)),
            pltpu.SemaphoreType.DMA((CHUNKS, 2)),
            pltpu.SemaphoreType.DMA((CHUNKS, 7)),
        ],
        compiler_params=pltpu.CompilerParams(
            collective_id=0, has_side_effects=True, vmem_limit_bytes=56 << 20
        ),
    )(
        old_experts,
        new_experts,
        new_experts.reshape(1, -1),
        cache_lengths.reshape(1, -1),
        sink_logits.reshape(1, -1),
        jnp.transpose(route_logits, (0, 2, 1)),
        jnp.transpose(routes, (0, 2, 1)),
        norm_gain,
        queries,
        cache_band,
        new_kv,
        o_weight.T,
        residual,
        train_gate_up,
        jnp.transpose(train_down, (1, 0, 2)),
    )
    return out, synced[None]


def solution(mesh):
    in_specs = (
        P(None, "expert", "head"),
        P("expert", None, "head"),
        P(None, "expert", "head"),
        P("expert"),
        P("head"),
        P("head", None),
        P(None, "expert", "head"),
        P(),
        P(None, "expert", None),
        P(None, "expert", None),
        P(),
        P(),
        P(None, "expert", None, "head"),
        P(None, "expert", "head"),
    )
    out_specs = (P(None, "expert", "head"), P("expert", None, "head"))
    body = functools.partial(local, mesh.shape["expert"], mesh.shape["head"])
    return jax.shard_map(body, mesh=mesh, in_specs=in_specs, out_specs=out_specs, check_vma=False)
```
